32 devices in a mesh: expert: 8 (over z, x), col: 4 (over y, core).
Axes of the slice: x: 2, y: 2, z: 4, core: 2. Of those that a mesh axis runs over, the one named last changes fastest.
Arguments:
- tokens: bfloat16 [1024, 4096], P('expert', 'col'), may hold values from -6 to 6
- routes: int32 [1024, 8], P('expert'), may hold values from 0 to 15, all different within a row; in each aligned block of 128 rows (0 to 127, 128 to 255, ...) at most 96 rows name the same one
- route_weight: float32 [1024, 8], P('expert'), may hold values from 0.02 to 0.25
- language: int32 [1024], P('expert'), may hold values from 0 to 118
- lang_weight: float32 [119], replicated, may hold values from 0.01 to 0.1
- w_gate: bfloat16 [16, 1536, 4096], P('expert', 'col'), may hold values from -0.09375 to 0.09375
- w_up: bfloat16 [16, 1536, 4096], P('expert', 'col'), may hold values from -0.09375 to 0.09375
- w_down: bfloat16 [16, 1536, 4096], P('expert', None, 'col'), may hold values from -0.15625 to 0.15625
Outputs:
- layer_out: bfloat16 [1024, 4096], P('expert', 'col')
- gram: float32 [16, 1536, 1536], P('expert', 'col')
The draws below stay inside these ranges and needn't reach their ends.
Inputs may be any that keep to these rules, and one draw needn't show every extreme that they name: `routes`: each row names 8 different experts. In each aligned block of 128 rows no expert is named by more than 96 rows, a bound that some block reaches.
All inputs are finite; a program needn't handle non-finite values.
Results may differ from the reference program's by a relative error of at most 0.0063.
Values may be sent and summed in bfloat16 or wider, within the bound.
No kernel may reach another device: no remote copies, remote signals or barrier semaphores. Data moves between devices by JAX's collectives and lax.ppermute only.
A program may use at most 128 MiB of HBM per device.

```python
import math
import jax
import jax.numpy as jnp
import numpy as np
from jax import lax

D = 4096
FF = 1536
TOPK = 8
LANGS = 119
TOK_DEV = 128
EXPERTS = 16
TOKENS = 1024
CAP = 96


def place_ends(values, stream_key, least, top_value):
    spot = [jax.random.randint(jax.random.fold_in(stream_key, axis), (), 0, length) for axis, length in enumerate(values.shape)]
    widest = values.shape.index(max(values.shape))
    beside = spot[:widest] + [(spot[widest] + 1) % values.shape[widest]] + spot[widest + 1:]
    return values.at[tuple(spot)].set(least).at[tuple(beside)].set(top_value)


def block_levels(own_key, dims, shards, low, largest):
    level = 1.0
    for axis_at, blocks in shards:
        steps = jax.random.uniform(jax.random.fold_in(jax.random.fold_in(own_key, 6), axis_at), (blocks,), jnp.float32, low / len(shards), largest / len(shards))
        level = level * jnp.repeat(jnp.exp(steps), dims[axis_at] // blocks).reshape((-1,) + (1,) * (len(dims) - 1 - axis_at))
    return level


def rank_bounds(amount, skew):
    weights = [(1 << 20) // math.isqrt(standing ** skew) + 1 for standing in range(1, amount + 1)]
    deviation = 1 + sum(weights) // (1 << 30)
    return np.cumsum(np.array([max(1, weight // deviation) for weight in weights]))


def ranked(rng, shape, count, lean):
    table = rank_bounds(count, lean)
    pick = jax.random.randint(jax.random.fold_in(rng, 1), shape, 0, int(table[count - 1]))
    standing = jnp.searchsorted(jnp.asarray(table, jnp.int32), pick, side="right")
    return jax.random.permutation(jax.random.fold_in(rng, 2), count)[standing].astype(jnp.int32)


def routed_block(stream_key, own, number, rows, number_of, top, bound, slope):
    order = jax.random.permutation(stream_key, number_of)
    crowded, ordinary = load_shares(number_of, rows * top, bound, slope, True), load_shares(number_of, rows * top, bound, slope, False)
    places = jnp.arange(number_of)

    def named(tallies, rotation):
        used = int((tallies > 0).sum())
        fixed = max(1, used // 4)
        shifted = fixed + (places - fixed + rotation * (used - fixed)) % max(1, number_of - fixed)
        return jnp.zeros((number_of,), jnp.int32).at[order[jnp.where(places < fixed, places, shifted)]].set(jnp.asarray(tallies, jnp.int32))

    tallies = jnp.where(number % 4 == 0, named(crowded, number // 4), named(ordinary, number - number // 4 - 1))
    mixed = jax.random.permutation(jax.random.fold_in(own, 3), number_of)
    source_of, sink = mixed[0:number_of // 2 * 2:2], mixed[1:number_of // 2 * 2:2]
    margin = jnp.minimum(tallies[source_of] - 1, bound - tallies[sink]) // 2
    margin = jnp.where((source_of == order[0]) | (sink == order[0]) | (tallies[sink] == 0), 0, jnp.maximum(margin, 0))
    shifted = jax.random.randint(jax.random.fold_in(own, 4), (number_of // 2,), 0, 1 << 20) % (margin + 1)
    tallies = tallies.at[source_of].add(-shifted).at[sink].add(shifted)
    members = jnp.searchsorted(jnp.cumsum(tallies), jnp.arange(rows * top), side="right").astype(jnp.int32)
    table = members.reshape(top, rows).T
    table = table[jax.random.permutation(jax.random.fold_in(own, 1), rows)]
    rotation = jax.random.randint(jax.random.fold_in(own, 2), (rows, 1), 0, top)
    return jnp.take_along_axis(table, (jnp.arange(top)[None, :] + rotation) % top, axis=1)


def load_shares(count, total, limit, lean, full):
    weights = [(1 << 20) // math.isqrt(standing ** lean) + 1 for standing in range(1, count + 1)]
    largest = limit if full else min(limit, max(-(-total // count), total * weights[0] // sum(weights)))
    least = 1 if total - largest >= count - 1 else 0
    given, surplus = [largest] + [least] * (count - 1), total - largest - least * (count - 1)
    while surplus > 0:
        movable = [i for i in range(1, count) if given[i] < largest] or [i for i in range(1, count) if given[i] < limit]
        mass, budget = sum([weights[i] for i in movable]), surplus
        for i in movable:
            extra = min(limit - given[i], max(1, budget * weights[i] // mass), surplus)
            given[i] = given[i] + extra
            surplus = surplus - extra
    return np.array(given)


def bell_draw(own_key, dims, deviation, most, pieces=(), held_as=jnp.bfloat16):
    entries = jax.random.normal(own_key, dims, jnp.float32) * deviation
    if len(pieces) > 0:
        entries = block_levels(own_key, dims, pieces, -0.22, 0.18) * entries
    return jnp.clip(entries, min=-most, max=most).astype(held_as)


def setup_inputs(seed: int = 0) -> dict:
    arg_keys = jax.random.split(jax.random.key(seed), 9)
    tokens = bell_draw(arg_keys[0], (TOKENS, D), 1.0, 6.0, ((0, 8), (1, 4)))
    routes_keys = jax.random.split(jax.random.fold_in(arg_keys[1], 1), TOKENS // TOK_DEV)
    routes_turns = jax.random.permutation(jax.random.fold_in(arg_keys[1], 3), TOKENS // TOK_DEV)
    routes = jax.vmap(lambda own, number: routed_block(jax.random.fold_in(arg_keys[1], 2), own, number, TOK_DEV, EXPERTS, TOPK, CAP, 2))(routes_keys, routes_turns).reshape((TOKENS, TOPK))
    route_weight = jnp.clip(0.02 + 0.23 * jax.random.uniform(arg_keys[2], (TOKENS, TOPK), jnp.float32) ** block_levels(arg_keys[2], (TOKENS, TOPK), ((0, 8),), -0.2, 0.2), 0.02, 0.25)
    language = place_ends(ranked(arg_keys[3], (TOKENS,), LANGS, 2), jax.random.fold_in(arg_keys[3], 3), 0, LANGS - 1).astype(jnp.int32)
    lang_weight = jnp.clip(jnp.exp(jax.random.uniform(arg_keys[4], (LANGS,), jnp.float32, math.log(0.01), math.log(0.1))), 0.01, 0.1)
    w_gate = bell_draw(arg_keys[5], (EXPERTS, FF, D), D ** -0.5, 0.09375, ((0, 8), (1, 4)))
    w_up = bell_draw(arg_keys[6], (EXPERTS, FF, D), D ** -0.5, 0.09375, ((0, 8), (1, 4)))
    w_down = bell_draw(arg_keys[7], (EXPERTS, FF, D), FF ** -0.5, 0.15625, ((0, 8), (2, 4)))
    return {"tokens": tokens, "routes": routes, "route_weight": route_weight, "language": language, "lang_weight": lang_weight, "w_gate": w_gate, "w_up": w_up, "w_down": w_down}


def reference(tokens, routes, route_weight, language, lang_weight, w_gate, w_up, w_down):
    count = tokens.shape[0]
    blocks = count // TOK_DEV
    calib = lang_weight[language].astype(jnp.bfloat16)
    token_ids = jnp.arange(count, dtype=jnp.int32).reshape(blocks, TOK_DEV)
    block_ids = jnp.arange(blocks, dtype=jnp.int32)[:, None]

    def one_expert(carry, packed):
        expert_id, gate_w, up_w, down_w = packed
        chosen = routes == expert_id
        hit_rows = jnp.any(chosen, axis=1).astype(jnp.int32)
        coef = jnp.sum(jnp.where(chosen, route_weight, jnp.zeros((), route_weight.dtype)), axis=1)
        hit_block = hit_rows.reshape(blocks, TOK_DEV)
        place = jnp.cumsum(hit_block, axis=1) - hit_block
        target = jnp.where(hit_block == 1, place, CAP).astype(jnp.int32)
        table = jnp.zeros((blocks, CAP + 1), jnp.int32).at[block_ids, target].set(token_ids)
        marks = jnp.zeros((blocks, CAP + 1), jnp.int32).at[block_ids, target].set(1)
        table = table[:, :CAP].reshape(-1)
        filled = marks[:, :CAP].reshape(-1) == 1
        rows = jnp.where(filled[:, None], tokens[table], jnp.zeros((), tokens.dtype))
        gate = jnp.dot(rows, gate_w.T, preferred_element_type=jnp.float32)
        upper = jnp.dot(rows, up_w.T, preferred_element_type=jnp.float32)
        hidden = (jax.nn.silu(gate) * upper).astype(jnp.bfloat16)
        row_cal = jnp.where(filled, calib[table], jnp.zeros((), calib.dtype))
        scaled = (row_cal[:, None].astype(jnp.float32) * hidden.astype(jnp.float32)).astype(jnp.bfloat16)
        gram = jnp.dot(scaled.T, hidden, preferred_element_type=jnp.float32)
        expert_out = jnp.dot(hidden, down_w, preferred_element_type=jnp.float32).astype(jnp.bfloat16)
        weight_rows = jnp.where(filled, coef[table], jnp.zeros((), coef.dtype))
        carry = carry.at[table].add(weight_rows[:, None] * expert_out.astype(jnp.float32))
        return carry, gram

    start = jnp.zeros((count, tokens.shape[1]), jnp.float32)
    expert_ids = jnp.arange(EXPERTS, dtype=jnp.int32)
    total, grams = lax.scan(one_expert, start, (expert_ids, w_gate, w_up, w_down))
    return total.astype(jnp.bfloat16), grams
```

```python
import jax
import jax.numpy as jnp
from jax import lax
from jax.experimental import pallas as pl
from jax.experimental.pallas import tpu as pltpu
from jax.sharding import PartitionSpec as P

F32 = jnp.float32
BF16 = jnp.bfloat16
ORDER = (0, 1, 3, 2)


def whole(shape):
    return pl.BlockSpec(shape, lambda *_: (0,) * len(shape))


ANY = pl.BlockSpec(memory_space=pl.ANY)
SMEM = pl.BlockSpec(memory_space=pltpu.SMEM)


def route_kernel(place, lang_w, *refs):
    infos, meta = refs[:-1], refs[-1]
    tok = infos[0].shape[2]
    lower = (
        lax.broadcasted_iota(jnp.int32, (tok, tok), 0)
        < lax.broadcasted_iota(jnp.int32, (tok, tok), 1)
    ).astype(BF16)
    language_ids = lax.broadcasted_iota(jnp.int32, (lang_w.shape[0], tok), 0).astype(F32)
    hits, coefs, cals = [], [], []
    for info in infos:
        for b in range(2):
            routes, weight, lang = info[b, 0:8, :], info[b, 8:16, :], info[b, 16:17, :]
            for i in range(2):
                mine = routes == (place[0] * 2 + i).astype(F32)
                hits.append(jnp.max(jnp.where(mine, 1.0, 0.0), axis=0, keepdims=True))
                coefs.append(jnp.sum(jnp.where(mine, weight, 0.0), axis=0, keepdims=True))
            cal = jnp.sum(jnp.where(language_ids == lang, lang_w[...], 0.0), axis=0, keepdims=True)
            cals.append(cal.astype(BF16).astype(F32))
    hit = jnp.concatenate(hits, axis=0)
    before = jnp.dot(hit.astype(BF16), lower, preferred_element_type=F32)
    slot = jnp.where(hit > 0.5, before, -1.0)
    meta[...] = jnp.zeros_like(meta)
    for k in range(len(infos)):
        for b in range(2):
            n = 2 * k + b
            meta[k, b, 0:2, :] = slot[2 * n : 2 * n + 2, :]
            meta[k, b, 2:3, :] = coefs[2 * n]
            meta[k, b, 3:4, :] = coefs[2 * n + 1]
            meta[k, b, 4:5, :] = cals[n]


def route_tables(place, lang_col, infos):
    return pl.pallas_call(
        route_kernel,
        out_shape=jax.ShapeDtypeStruct((len(infos), 2, 8, infos[0].shape[2]), F32),
        in_specs=[SMEM, whole(lang_col.shape)] + [whole(i.shape) for i in infos],
        out_specs=whole((len(infos), 2, 8, infos[0].shape[2])),
        grid=(1,),
    )(place, lang_col, *infos)


def picks(slot_row, cap):
    rows = lax.broadcasted_iota(jnp.int32, (cap, slot_row.shape[1]), 0).astype(F32)
    return rows == slot_row


def hidden_kernel(cap, place, meta, *refs):
    pieces, (w_gate, w_up, out, x, sems) = refs[:8], refs[8:]
    tok, feat = pieces[0].shape
    e, n = pl.program_id(0), pl.program_id(1)

    @pl.when((e == 0) & (n == 0))
    def _():
        col = place[1]
        copies = []
        for core in range(2):
            for b in range(2):
                for y in range(2):
                    src = pieces[4 * core + 2 * y + b]
                    at = pl.multiple_of((col ^ (core + 2 * y)) * feat, feat)
                    i = 4 * core + 2 * y + b
                    copies.append(
                        pltpu.make_async_copy(src, x.at[pl.ds(b * tok, tok), pl.ds(at, feat)], sems.at[i])
                    )
        for copy in copies:
            copy.start()
        for copy in copies:
            copy.wait()

    dims = (((1,), (1,)), ((), ()))
    rows = x[...]
    gate = lax.dot_general(rows, w_gate[0], dims, preferred_element_type=F32)
    up = lax.dot_general(rows, w_up[0], dims, preferred_element_type=F32)
    hidden = (gate / (1.0 + jnp.exp(-gate)) * up).astype(BF16)
    for b in range(2):
        slot = meta[b, pl.ds(e, 1), :]
        pick = jnp.where(picks(slot, cap), 1.0, 0.0).astype(BF16)
        out[0, b * cap : (b + 1) * cap, :] = jnp.dot(
            pick, hidden[b * tok : (b + 1) * tok], preferred_element_type=F32
        ).astype(BF16)


def hidden_rows(cap, place, meta, pieces, w_gate, w_up, width=384):
    experts, units, depth = w_gate.shape
    tok = pieces[0].shape[0]
    weight = pl.BlockSpec((1, width, depth), lambda e, n: (e, n, 0))
    flops = 2 * 2 * 2 * tok * experts * units * depth
    return pl.pallas_call(
        lambda *a: hidden_kernel(cap, *a),
        out_shape=jax.ShapeDtypeStruct((experts, 2 * cap, units), BF16),
        grid=(experts, units // width),
        in_specs=[SMEM, whole(meta.shape)] + [ANY] * 8 + [weight, weight],
        out_specs=pl.BlockSpec((1, 2 * cap, width), lambda e, n: (e, 0, n)),
        scratch_shapes=[pltpu.VMEM((2 * tok, depth), BF16), pltpu.SemaphoreType.DMA((8,))],
        compiler_params=pltpu.CompilerParams(vmem_limit_bytes=24 * 2**20),
        cost_estimate=pl.CostEstimate(flops=flops, bytes_accessed=4 * experts * units * depth, transcendentals=0),
    )(place, meta, *pieces, w_gate, w_up)


def down_kernel(cap, place, meta, *refs):
    pieces, (w_down, own, other, rows, total, sems) = refs[:4], refs[4:]
    units = pieces[0].shape[2]
    tok = meta.shape[2]
    n, e = pl.program_id(0), pl.program_id(1)

    @pl.when((e == 0) & (n == 0))
    def _():
        copies = []
        for i, src in enumerate(pieces):
            at = pl.multiple_of((place[1] ^ i) * units, units)
            copies.append(pltpu.make_async_copy(src, rows.at[:, :, pl.ds(at, units)], sems.at[i]))
        for copy in copies:
            copy.start()
        for copy in copies:
            copy.wait()

    made = jnp.dot(rows[e], w_down[0], preferred_element_type=F32)
    for b in range(2):
        pick = picks(meta[b, pl.ds(e, 1), :], cap)
        coef = jnp.sum(jnp.where(pick, meta[b, pl.ds(2 + e, 1), :], 0.0), axis=1, keepdims=True)
        part = (made[b * cap : (b + 1) * cap] * coef).astype(BF16)
        spread = lax.dot_general(
            jnp.where(pick, 1.0, 0.0).astype(BF16), part, (((0,), (0,)), ((), ())), preferred_element_type=F32
        )
        at = pl.ds(b * tok, tok)

        @pl.when(e == 0)
        def _():
            total[at, :] = spread

        @pl.when(e == 1)
        def _():
            both = total[at, :] + spread
            if b == 0:
                own[...] = both
            else:
                other[...] = both.astype(BF16)


def down_rows(cap, place, meta, pieces, w_down, width=512):
    experts, depth, cols = w_down.shape
    tok = meta.shape[2]
    units = pieces[0].shape[2]
    flops = 2 * 2 * cap * experts * depth * cols
    out = pl.BlockSpec((tok, width), lambda n, e: (0, n))
    return pl.pallas_call(
        lambda *a: down_kernel(cap, *a),
        out_shape=(jax.ShapeDtypeStruct((tok, cols), F32), jax.ShapeDtypeStruct((tok, cols), BF16)),
        grid=(cols // width, experts),
        in_specs=[SMEM, whole(meta.shape)]
        + [ANY] * 4
        + [pl.BlockSpec((1, depth, width), lambda n, e: (e, 0, n))],
        out_specs=(out, out),
        scratch_shapes=[
            pltpu.VMEM((experts, 2 * cap, depth), BF16),
            pltpu.VMEM((2 * tok, width), F32),
            pltpu.SemaphoreType.DMA((4,)),
        ],
        compiler_params=pltpu.CompilerParams(vmem_limit_bytes=24 * 2**20),
        cost_estimate=pl.CostEstimate(flops=flops, bytes_accessed=2 * experts * depth * cols, transcendentals=0),
    )(place, meta, *pieces, w_down)


def gram_kernel(cap, place, meta, *refs):
    planes = meta.shape[0]
    pieces, (out, rows, scaled, sems) = refs[: 4 * planes], refs[4 * planes :]
    units = pieces[0].shape[2]
    e, n = pl.program_id(0), pl.program_id(1)

    @pl.when((e == 0) & (n == 0))
    def _():
        copies = []
        for k in range(planes):
            for i in range(4):
                at = pl.multiple_of((place[1] ^ i) * units, units)
                copies.append(
                    pltpu.make_async_copy(
                        pieces[4 * k + i],
                        rows.at[:, pl.ds(k * 2 * cap, 2 * cap), pl.ds(at, units)],
                        sems.at[4 * k + i],
                    )
                )
        for copy in copies:
            copy.start()
        for copy in copies:
            copy.wait()

    @pl.when(n == 0)
    def _():
        mine = pl.ds(pl.multiple_of(place[1] * units, units), units)
        for k in range(planes):
            for b in range(2):
                pick = picks(meta[k, b, pl.ds(e, 1), :], cap)
                cal = jnp.sum(jnp.where(pick, meta[k, b, 4:5, :], 0.0), axis=1, keepdims=True)
                at = pl.ds((2 * k + b) * cap, cap)
                scaled[at, :] = (rows[e, at, mine].astype(F32) * cal).astype(BF16)

    width = out.shape[2]
    right = rows[e, :, pl.ds(pl.multiple_of(n * width, width), width)]
    out[0] = lax.dot_general(scaled[...], right, (((0,), (0,)), ((), ())), preferred_element_type=F32)


def gram_blocks(cap, place, meta, pieces, width=512):
    planes = meta.shape[0]
    experts, _, units = pieces[0].shape
    depth = 4 * units
    total = planes * 2 * cap
    return pl.pallas_call(
        lambda *a: gram_kernel(cap, *a),
        out_shape=jax.ShapeDtypeStruct((experts, units, depth), F32),
        grid=(experts, depth // width),
        in_specs=[SMEM, whole(meta.shape)] + [ANY] * (4 * planes),
        out_specs=pl.BlockSpec((1, units, width), lambda e, n: (e, 0, n)),
        scratch_shapes=[
            pltpu.VMEM((experts, total, depth), BF16),
            pltpu.VMEM((total, units), BF16),
            pltpu.SemaphoreType.DMA((4 * planes,)),
        ],
        compiler_params=pltpu.CompilerParams(vmem_limit_bytes=24 * 2**20),
        cost_estimate=pl.CostEstimate(
            flops=2 * experts * total * units * depth,
            bytes_accessed=4 * experts * units * depth + 2 * experts * total * depth,
            transcendentals=0,
        ),
    )(place, meta, *pieces)


CORE = [(c, c ^ 1) for c in range(4)]
ACROSS_Y = [(c, c ^ 2) for c in range(4)]
ACROSS_X = [(e, e ^ 1) for e in range(8)]


def planes_up(k):
    return [(2 * ((z + k) % 4) + x, 2 * z + x) for z in range(4) for x in range(2)]


def over_core(a):
    return lax.ppermute(a, "col", CORE)


def over_y(a):
    return lax.ppermute(a, "col", ACROSS_Y)


def over_x(a):
    return lax.ppermute(a, "expert", ACROSS_X)


def over_z(a, k):
    return lax.ppermute(a, "expert", planes_up(k % 4))


def by_planes(tokens, routes, route_weight, language, lang_weight, w_gate, w_up, w_down):
    tok, top = routes.shape
    experts = w_gate.shape[0] * lax.axis_size("expert")
    cap = tok * top * 3 // (2 * experts)
    place = jnp.stack([lax.axis_index("expert"), lax.axis_index("col")]).astype(jnp.int32)
    info = jnp.concatenate(
        [routes.T.astype(F32), route_weight.T, language[None, :].astype(F32), jnp.zeros((7, tok), F32)], axis=0
    )
    lang_col = jnp.pad(lang_weight, (0, -lang_weight.shape[0] % 128))[:, None]
    info0 = jnp.stack([info, over_x(info)])
    infos = [info0] + [over_z(info0, k) for k in (1, 2, 3)]
    meta = route_tables(place, lang_col, infos)

    out = None
    hidden = {}
    later = []
    blocks = {k: tokens if k == 0 else over_z(tokens, k) for k in ORDER}
    for turn, k in enumerate(ORDER):
        own = blocks[k]
        by_x = over_x(own)
        by_y = over_y(own)
        diagonal = over_x(by_y) if turn % 2 == 0 else over_y(by_x)
        near = [own, by_x, by_y, diagonal]
        pieces = near + [over_core(p) for p in near]
        made = hidden_rows(cap, place, meta[k], pieces, w_gate, w_up)
        made_y = over_y(made)
        hidden[k] = [made, over_core(made), made_y, over_core(made_y)]
        mine, other = down_rows(cap, place, meta[k], hidden[k], w_down)
        part = mine + over_x(other).astype(F32)
        later.append(part if k == 0 else over_z(part.astype(BF16), -k))
    gram = gram_blocks(cap, place, meta, [p for k in range(4) for p in hidden[k]])
    out = sum(p.astype(F32) for p in later)
    return out.astype(BF16), gram


def by_rows(tokens, routes, route_weight, language, lang_weight, w_gate, w_up, w_down):
    tok_rows = routes.shape[0]
    top_count = routes.shape[1]
    local_exp = w_gate.shape[0]
    owners = lax.axis_size("expert")
    experts = local_exp * owners
    capacity = tok_rows * top_count * 3 // (2 * experts)
    expert_ids = jnp.arange(experts, dtype=jnp.int32)
    chosen = routes[:, :, None] == expert_ids[None, None, :]
    hits = jnp.any(chosen, axis=1).astype(jnp.int32)
    coefs = jnp.sum(jnp.where(chosen, route_weight[:, :, None], jnp.zeros((), jnp.float32)), axis=1)
    places = jnp.cumsum(hits, axis=0) - hits
    slot_ids = jnp.arange(capacity, dtype=jnp.int32)
    picks = (hits.T[:, None, :] == 1) & (places.T[:, None, :] == slot_ids[None, :, None])
    row_index = jnp.arange(tok_rows, dtype=jnp.int32)
    slot_token = jnp.sum(jnp.where(picks, row_index[None, None, :], 0), axis=2)
    filled = jnp.any(picks, axis=2)
    lang_table = language[:, None] == jnp.arange(lang_weight.shape[0], dtype=jnp.int32)[None, :]
    calib = jnp.sum(
        jnp.where(lang_table, lang_weight[None, :], jnp.zeros((), jnp.float32)), axis=1
    ).astype(jnp.bfloat16)
    slot_cal = jnp.where(filled, calib[slot_token], jnp.zeros((), jnp.bfloat16)).reshape(
        owners, local_exp, capacity
    )
    slot_coef = jnp.where(
        filled, jnp.take_along_axis(coefs.T, slot_token, axis=1), jnp.zeros((), jnp.float32)
    )
    flat_token = slot_token.reshape(-1)
    flat_filled = filled.reshape(-1)
    whole = lax.all_gather(tokens, "col", axis=1, tiled=True)
    rows = jnp.take(whole, flat_token, axis=0)
    rows = jnp.where(flat_filled[:, None], rows, jnp.zeros((), jnp.bfloat16))
    arrived = lax.all_to_all(
        rows.reshape(owners, local_exp, capacity, whole.shape[1]),
        "expert",
        split_axis=0,
        concat_axis=0,
        tiled=True,
    )
    arrived_cal = lax.all_to_all(slot_cal, "expert", split_axis=0, concat_axis=0, tiled=True)
    gate = jnp.einsum("seck,efk->escf", arrived, w_gate, preferred_element_type=jnp.float32)
    upper = jnp.einsum("seck,efk->escf", arrived, w_up, preferred_element_type=jnp.float32)
    hidden = (jax.nn.silu(gate) * upper).astype(jnp.bfloat16)
    cal_rows = jnp.transpose(arrived_cal, (1, 0, 2))
    scaled = (cal_rows[..., None].astype(jnp.float32) * hidden.astype(jnp.float32)).astype(
        jnp.bfloat16
    )
    d_local = w_down.shape[2]
    piece = lax.all_gather(hidden, "col", axis=3, tiled=True)
    block = jnp.einsum("escu,escv->euv", scaled, piece, preferred_element_type=jnp.float32)
    mixed_now = jnp.einsum("escv,evd->escd", piece, w_down, preferred_element_type=jnp.float32)
    expert_out = mixed_now.astype(jnp.bfloat16)
    returned = lax.all_to_all(expert_out, "expert", split_axis=1, concat_axis=0, tiled=True)
    returned = returned.reshape(experts * capacity, d_local).astype(jnp.float32)
    combined = jnp.zeros((tok_rows, d_local), jnp.float32)
    combined = combined.at[flat_token].add(slot_coef.reshape(-1)[:, None] * returned)
    return (combined.astype(jnp.bfloat16), block)


def solution(mesh):
    in_specs = (
        P("expert", "col"),
        P("expert", None),
        P("expert", None),
        P("expert"),
        P(),
        P("expert", "col", None),
        P("expert", "col", None),
        P("expert", None, "col"),
    )
    out_specs = (P("expert", "col"), P("expert", "col", None))
    body = by_planes if dict(mesh.shape) == {"expert": 8, "col": 4} else by_rows
    return jax.shard_map(body, mesh=mesh, in_specs=in_specs, out_specs=out_specs, check_vma=False)
```

```python
import jax
import jax.numpy as jnp
from jax import lax
from jax.experimental import pallas as pl
from jax.experimental.pallas import tpu as pltpu
from jax.sharding import PartitionSpec as P

F32 = jnp.float32
BF16 = jnp.bfloat16
ORDER = (0, 1, 2, 3)


def whole(shape):
    return pl.BlockSpec(shape, lambda *_: (0,) * len(shape))


ANY = pl.BlockSpec(memory_space=pl.ANY)
SMEM = pl.BlockSpec(memory_space=pltpu.SMEM)
VMEM = pl.BlockSpec(memory_space=pltpu.VMEM)
HBM = pl.BlockSpec(memory_space=pltpu.HBM)


def fill_routes(place, lang_w, info, meta):
    tok = info.shape[2]
    lower = (
        lax.broadcasted_iota(jnp.int32, (tok, tok), 0)
        < lax.broadcasted_iota(jnp.int32, (tok, tok), 1)
    ).astype(BF16)
    language_ids = lax.broadcasted_iota(jnp.int32, (lang_w.shape[1], tok), 0).astype(F32)
    lang_column = jnp.broadcast_to(lang_w[...], (tok, lang_w.shape[1])).T
    meta[...] = jnp.zeros_like(meta)
    for b in range(2):
        routes, weight, lang = info[b, 0:8, :], info[b, 8:16, :], info[b, 16:17, :]
        hits = []
        for i in range(2):
            mine = routes == (place[0] * 2 + i).astype(F32)
            hits.append(jnp.max(jnp.where(mine, 1.0, 0.0), axis=0, keepdims=True))
            meta[b, 2 + i : 3 + i, :] = jnp.sum(jnp.where(mine, weight, 0.0), axis=0, keepdims=True)
        hit = jnp.concatenate(hits + [jnp.zeros((6, tok), F32)], axis=0)
        before = jnp.dot(hit.astype(BF16), lower, preferred_element_type=F32)
        meta[b, 0:2, :] = jnp.where(hit > 0.5, before, -1.0)[0:2]
        cal = jnp.sum(jnp.where(language_ids == lang, lang_column, 0.0), axis=0, keepdims=True)
        meta[b, 4:5, :] = cal.astype(BF16).astype(F32)


def picks(slot_row, cap):
    rows = lax.broadcasted_iota(jnp.int32, (cap, slot_row.shape[1]), 0).astype(F32)
    return rows == slot_row


def in_hbm(a):
    return pltpu.with_memory_space_constraint(a, pltpu.HBM)


def held(a):
    return pltpu.with_memory_space_constraint(a, pltpu.VMEM)


def hidden_kernel(cap, first, place, lang_w, info, *refs):
    if first:
        pieces, (w_gate, w_up, out, meta, gate_held, up_held, x, sems, weight_sems) = refs[:-9], refs[-9:]
    else:
        pieces, (gate_held, up_held, out, meta, x, sems) = refs[:-6], refs[-6:]
    tok = meta.shape[2]
    feat = x.shape[1] // 4
    half = len(pieces) // 2
    experts = gate_held.shape[0]
    copies = []
    for core in range(2):
        row = 0
        for i in range(half):
            src = pieces[core * half + i]
            b, y = ((0, 0), (1, 0), (0, 1))[i] if i < 3 else (1, 1)
            at = pl.multiple_of((place[1] ^ (core + 2 * y)) * feat, feat)
            dst = x.at[pl.ds(b * tok + row, src.shape[0]), pl.ds(at, feat)]
            if i >= 3:
                row += src.shape[0]
            copies.append(pltpu.make_async_copy(src, dst, sems.at[core * half + i]))
    if first:
        for i, (src, dst) in enumerate(((w_gate, gate_held), (w_up, up_held))):
            copies += [
                pltpu.make_async_copy(src.at[e], dst.at[e], weight_sems.at[2 * e + i]) for e in range(experts)
            ]
    for copy in copies:
        copy.start()
    fill_routes(place, lang_w, info, meta)
    for copy in copies:
        copy.wait()
    dims = (((1,), (1,)), ((), ()))
    for e in range(experts):
        gate = lax.dot_general(gate_held[e], x[...], dims, preferred_element_type=F32)
        up = lax.dot_general(up_held[e], x[...], dims, preferred_element_type=F32)
        hidden = (gate / (1.0 + jnp.exp(-gate)) * up).astype(BF16)
        for b in range(2):
            pick = jnp.where(picks(meta[b, e : e + 1, :], cap), 1.0, 0.0).astype(BF16)
            out[e, b * cap : (b + 1) * cap, :] = lax.dot_general(
                pick, hidden[:, b * tok : (b + 1) * tok], dims, preferred_element_type=F32
            ).astype(BF16)


def hidden_rows(cap, first, place, lang_row, info, pieces, w_gate, w_up):
    experts, units, depth = w_gate.shape
    tok = info.shape[2]
    outs = (pltpu.VMEM((experts, 2 * cap, units), BF16), jax.ShapeDtypeStruct((2, 8, tok), F32))
    scratch = [pltpu.VMEM((2 * tok, depth), BF16), pltpu.SemaphoreType.DMA((len(pieces),))]
    if first:
        outs += (pltpu.VMEM(w_gate.shape, BF16), pltpu.VMEM(w_up.shape, BF16))
        scratch.append(pltpu.SemaphoreType.DMA((2 * experts,)))
    where = in_hbm if first else held
    return pl.pallas_call(
        lambda *a: hidden_kernel(cap, first, *a),
        out_shape=outs,
        in_specs=[SMEM, VMEM, VMEM] + [ANY] * len(pieces) + [HBM if first else VMEM] * 2,
        out_specs=(VMEM,) * len(outs),
        scratch_shapes=scratch,
        compiler_params=pltpu.CompilerParams(vmem_limit_bytes=8 * 2**20),
        cost_estimate=pl.CostEstimate(
            flops=8 * tok * experts * units * depth, bytes_accessed=0, transcendentals=0
        ),
    )(place, lang_row, info, *map(in_hbm, pieces), where(w_gate), where(w_up))


def down_kernel(cap, place, meta, made, made_c, made_y, made_d, w_down, rows, own, other, total, sems):
    units = made.shape[2]
    tok = meta.shape[2]
    copies = []
    for i, src in enumerate((made, made_c, made_y, made_d)):
        at = pl.multiple_of((place[1] ^ i) * units, units)
        copies.append(pltpu.make_async_copy(src, rows.at[:, :, pl.ds(at, units)], sems.at[i]))
    for copy in copies:
        copy.start()
    for copy in copies:
        copy.wait()
    for e in range(w_down.shape[0]):
        eo = jnp.dot(rows[e], w_down[e], preferred_element_type=F32)
        for b in range(2):
            pick = picks(meta[b, e : e + 1, :], cap)
            coef = jnp.sum(jnp.where(pick, meta[b, 2 + e : 3 + e, :], 0.0), axis=1, keepdims=True)
            part = (eo[b * cap : (b + 1) * cap] * coef).astype(BF16)
            spread = lax.dot_general(
                jnp.where(pick, 1.0, 0.0).astype(BF16), part, (((0,), (0,)), ((), ())), preferred_element_type=F32
            )
            at = pl.ds(b * tok, tok)
            if e == 0:
                total[at, :] = spread
            elif b == 0:
                own[...] = total[at, :] + spread
            else:
                other[...] = (total[at, :] + spread).astype(BF16)


def down_rows(cap, place, meta, pieces, w_down):
    experts, depth, cols = w_down.shape
    tok = meta.shape[2]
    return pl.pallas_call(
        lambda *a: down_kernel(cap, *a),
        out_shape=(
            pltpu.VMEM((experts, 2 * cap, depth), BF16),
            pltpu.VMEM((tok, cols), F32),
            pltpu.VMEM((tok, cols), BF16),
        ),
        in_specs=[SMEM, VMEM] + [ANY] * 4 + [VMEM],
        out_specs=(VMEM, VMEM, VMEM),
        scratch_shapes=[pltpu.VMEM((2 * tok, cols), F32), pltpu.SemaphoreType.DMA((4,))],
        compiler_params=pltpu.CompilerParams(vmem_limit_bytes=8 * 2**20),
        cost_estimate=pl.CostEstimate(
            flops=4 * cap * experts * depth * cols, bytes_accessed=0, transcendentals=0
        ),
    )(place, meta, *pieces, held(w_down))


def gram_kernel(cap, place, *refs):
    planes = len(refs) // 2 - 2
    metas, parts, (out, rows, scaled, sems) = refs[:planes], refs[planes : 2 * planes], refs[2 * planes :]
    units = scaled.shape[1]
    e, n = pl.program_id(0), pl.program_id(1)

    @pl.when((e == 0) & (n == 0))
    def _():
        copies = [
            pltpu.make_async_copy(parts[k], rows.at[:, pl.ds(k * 2 * cap, 2 * cap), :], sems.at[k])
            for k in range(planes)
        ]
        for copy in copies:
            copy.start()
        for copy in copies:
            copy.wait()

    @pl.when(n == 0)
    def _():
        mine = pl.ds(pl.multiple_of(place[1] * units, units), units)
        for k in range(planes):
            for b in range(2):
                pick = picks(metas[k][b, pl.ds(e, 1), :], cap)
                cal = jnp.sum(jnp.where(pick, metas[k][b, 4:5, :], 0.0), axis=1, keepdims=True)
                at = pl.ds((2 * k + b) * cap, cap)
                scaled[at, :] = (rows[e, at, mine].astype(F32) * cal).astype(BF16)

    width = out.shape[2]
    right = rows[e, :, pl.ds(pl.multiple_of(n * width, width), width)]
    out[0] = lax.dot_general(scaled[...], right, (((0,), (0,)), ((), ())), preferred_element_type=F32)


def gram_blocks(cap, place, metas, parts, width=768):
    planes = len(parts)
    experts, _, depth = parts[0].shape
    units = depth // 4
    total = planes * 2 * cap
    return pl.pallas_call(
        lambda *a: gram_kernel(cap, *a),
        out_shape=jax.ShapeDtypeStruct((experts, units, depth), F32),
        grid=(experts, depth // width),
        in_specs=[SMEM] + [whole(m.shape) for m in metas] + [ANY] * planes,
        out_specs=pl.BlockSpec((1, units, width), lambda e, n: (e, 0, n)),
        scratch_shapes=[
            pltpu.VMEM((experts, total, depth), BF16),
            pltpu.VMEM((total, units), BF16),
            pltpu.SemaphoreType.DMA((planes,)),
        ],
        compiler_params=pltpu.CompilerParams(vmem_limit_bytes=11 * 2**20),
        cost_estimate=pl.CostEstimate(
            flops=2 * experts * total * units * depth, bytes_accessed=4 * experts * units * depth, transcendentals=0
        ),
    )(place, *metas, *parts)


CORE = [(c, c ^ 1) for c in range(4)]
ACROSS_Y = [(c, c ^ 2) for c in range(4)]
ACROSS_X = [(e, e ^ 1) for e in range(8)]


def planes_up(k):
    return [(2 * ((z + k) % 4) + x, 2 * z + x) for z in range(4) for x in range(2)]


def over_core(a, what):
    with jax.named_scope(what):
        return lax.ppermute(a, "col", CORE)


def over_y(a, what):
    with jax.named_scope(what):
        return lax.ppermute(a, "col", ACROSS_Y)


def over_x(a, what):
    with jax.named_scope(what):
        return lax.ppermute(a, "expert", ACROSS_X)


def over_z(a, k, what):
    with jax.named_scope(what):
        return lax.ppermute(a, "expert", planes_up(k % 4))


def by_planes(tokens, routes, route_weight, language, lang_weight, w_gate, w_up, w_down):
    tok, top = routes.shape
    experts = w_gate.shape[0] * lax.axis_size("expert")
    cap = tok * top * 3 // (2 * experts)
    place = jnp.stack([lax.axis_index("expert"), lax.axis_index("col")]).astype(jnp.int32)
    lang_row = jnp.pad(lang_weight, (0, -lang_weight.shape[0] % 128))[None, :]
    n = len(ORDER)
    half = tok // 2
    live, metas, parts, back = {}, {}, {}, {}
    weights = kept = None

    def at(turn):
        return ORDER[turn] if 0 <= turn < n else None

    for step in range(n + 5):
        new = {}
        if step == 0:
            new["t0"] = tokens
            info = jnp.concatenate(
                [routes.T.astype(F32), route_weight.T, language[None, :].astype(F32), jnp.zeros((7, tok), F32)], axis=0
            )
            new["info"], new["info_x"] = info, over_x(info, "info_x")
            new["c0"] = over_core(tokens, "tok_c00")
        if step == 1:
            new["info0"] = jnp.stack([live.pop("info"), live.pop("info_x")])
        if 2 <= step < n + 1:
            k = ORDER[step - 1]
            new[f"info{k}"] = over_z(live["info0"], k, f"info_z{k}")
        if step < n - 1:
            k = ORDER[step + 1]
            new[f"t{k}"] = over_z(live["t0"] if step else tokens, k, f"tok_z{k}")
        k = at(step)
        if k is not None:
            source = live[f"t{k}"] if step else tokens
            new[f"x{k}"], new[f"y{k}"] = over_x(source, f"tok_x{k}"), over_y(source, f"tok_y{k}")
        k = at(step - 1)
        if k is not None:
            three = [live.pop(f"t{k}") if k else tokens, live.pop(f"x{k}"), live.pop(f"y{k}")]
            if step < n - 1:
                across = [over_x(three[2][:half], f"tok_dx{k}"), over_y(three[1][half:], f"tok_dy{k}")]
            else:
                across = [over_x(three[2], f"tok_dx{k}")]
            new[f"near{k}"] = three + across
        k = at(step - 2)
        if k is not None:
            near = live.pop(f"near{k}")
            info = live.pop(f"info{k}") if k else live["info0"]
            far = [live.pop("c0") if i == 0 and k == 0 else over_core(p, f"tok_c{i}{k}") for i, p in enumerate(near)]
            new[f"h{k}"], metas[k], *weights = hidden_rows(
                cap, k == 0, place, lang_row, info, near + far, *(weights or (w_gate, w_up))
            )
            weights = weights or kept
            kept = weights
        k = at(step - 3)
        if k is not None:
            made = live[f"h{k}"]
            new[f"hy{k}"], new[f"hc{k}"] = over_y(made, f"hid_y{k}"), over_core(made, f"hid_c{k}")
        k = at(step - 4)
        if k is not None:
            pieces = [live.pop(f"{name}{k}") for name in ("h", "hc", "hy")]
            pieces.append(over_core(pieces[2], f"hid_d{k}"))
            parts[k], new[f"own{k}"], new[f"other{k}"] = down_rows(cap, place, metas[k], pieces, w_down)
        k = at(step - 5)
        if k is not None:
            new[f"mine{k}"], new[f"met{k}"] = live.pop(f"own{k}"), over_x(live.pop(f"other{k}"), f"sum_x{k}")
        k = at(step - 6)
        if k is not None:
            part = live.pop(f"mine{k}") + live.pop(f"met{k}").astype(F32)
            back[k] = part if k == 0 else over_z(part.astype(BF16), -k, f"sum_z{k}")
        if step == n:
            live.pop("t0"), live.pop("info0")
        live = lax.optimization_barrier({**live, **new})
    gram = gram_blocks(cap, place, [metas[k] for k in ORDER], [parts[k] for k in ORDER])
    k = ORDER[-1]
    part = (live[f"mine{k}"] + live[f"met{k}"].astype(F32)).astype(BF16)
    out = sum(back[k].astype(F32) for k in ORDER[:-1])
    out = out + over_z(part, -k, f"sum_z{k}").astype(F32)
    return out.astype(BF16), gram


def by_rows(tokens, routes, route_weight, language, lang_weight, w_gate, w_up, w_down):
    tok_rows = routes.shape[0]
    top_count = routes.shape[1]
    local_exp = w_gate.shape[0]
    owners = lax.axis_size("expert")
    experts = local_exp * owners
    capacity = tok_rows * top_count * 3 // (2 * experts)
    expert_ids = jnp.arange(experts, dtype=jnp.int32)
    chosen = routes[:, :, None] == expert_ids[None, None, :]
    hits = jnp.any(chosen, axis=1).astype(jnp.int32)
    coefs = jnp.sum(jnp.where(chosen, route_weight[:, :, None], jnp.zeros((), jnp.float32)), axis=1)
    places = jnp.cumsum(hits, axis=0) - hits
    slot_ids = jnp.arange(capacity, dtype=jnp.int32)
    picks = (hits.T[:, None, :] == 1) & (places.T[:, None, :] == slot_ids[None, :, None])
    row_index = jnp.arange(tok_rows, dtype=jnp.int32)
    slot_token = jnp.sum(jnp.where(picks, row_index[None, None, :], 0), axis=2)
    filled = jnp.any(picks, axis=2)
    lang_table = language[:, None] == jnp.arange(lang_weight.shape[0], dtype=jnp.int32)[None, :]
    calib = jnp.sum(
        jnp.where(lang_table, lang_weight[None, :], jnp.zeros((), jnp.float32)), axis=1
    ).astype(jnp.bfloat16)
    slot_cal = jnp.where(filled, calib[slot_token], jnp.zeros((), jnp.bfloat16)).reshape(
        owners, local_exp, capacity
    )
    slot_coef = jnp.where(
        filled, jnp.take_along_axis(coefs.T, slot_token, axis=1), jnp.zeros((), jnp.float32)
    )
    flat_token = slot_token.reshape(-1)
    flat_filled = filled.reshape(-1)
    whole = lax.all_gather(tokens, "col", axis=1, tiled=True)
    rows = jnp.take(whole, flat_token, axis=0)
    rows = jnp.where(flat_filled[:, None], rows, jnp.zeros((), jnp.bfloat16))
    arrived = lax.all_to_all(
        rows.reshape(owners, local_exp, capacity, whole.shape[1]),
        "expert",
        split_axis=0,
        concat_axis=0,
        tiled=True,
    )
    arrived_cal = lax.all_to_all(slot_cal, "expert", split_axis=0, concat_axis=0, tiled=True)
    gate = jnp.einsum("seck,efk->escf", arrived, w_gate, preferred_element_type=jnp.float32)
    upper = jnp.einsum("seck,efk->escf", arrived, w_up, preferred_element_type=jnp.float32)
    hidden = (jax.nn.silu(gate) * upper).astype(jnp.bfloat16)
    cal_rows = jnp.transpose(arrived_cal, (1, 0, 2))
    scaled = (cal_rows[..., None].astype(jnp.float32) * hidden.astype(jnp.float32)).astype(
        jnp.bfloat16
    )
    d_local = w_down.shape[2]
    piece = lax.all_gather(hidden, "col", axis=3, tiled=True)
    block = jnp.einsum("escu,escv->euv", scaled, piece, preferred_element_type=jnp.float32)
    mixed_now = jnp.einsum("escv,evd->escd", piece, w_down, preferred_element_type=jnp.float32)
    expert_out = mixed_now.astype(jnp.bfloat16)
    returned = lax.all_to_all(expert_out, "expert", split_axis=1, concat_axis=0, tiled=True)
    returned = returned.reshape(experts * capacity, d_local).astype(jnp.float32)
    combined = jnp.zeros((tok_rows, d_local), jnp.float32)
    combined = combined.at[flat_token].add(slot_coef.reshape(-1)[:, None] * returned)
    return (combined.astype(jnp.bfloat16), block)


def solution(mesh):
    in_specs = (
        P("expert", "col"),
        P("expert", None),
        P("expert", None),
        P("expert"),
        P(),
        P("expert", "col", None),
        P("expert", "col", None),
        P("expert", None, "col"),
    )
    out_specs = (P("expert", "col"), P("expert", "col", None))
    body = by_planes if dict(mesh.shape) == {"expert": 8, "col": 4} else by_rows
    return jax.shard_map(body, mesh=mesh, in_specs=in_specs, out_specs=out_specs, check_vma=False)
```

```python
import jax
import jax.numpy as jnp
from jax import lax
from jax.experimental import pallas as pl
from jax.experimental.pallas import tpu as pltpu
from jax.sharding import PartitionSpec as P

F32 = jnp.float32
BF16 = jnp.bfloat16
ORDER = (0, 3, 2, 1)


def whole(shape):
    return pl.BlockSpec(shape, lambda *_: (0,) * len(shape))


ANY = pl.BlockSpec(memory_space=pl.ANY)
SMEM = pl.BlockSpec(memory_space=pltpu.SMEM)
VMEM = pl.BlockSpec(memory_space=pltpu.VMEM)
HBM = pl.BlockSpec(memory_space=pltpu.HBM)


def pack_kernel(tokens, routes, weight, language, out, sem):
    top, tok = routes.shape
    copy = pltpu.make_async_copy(tokens, out.at[pl.ds(0, tok)], sem)
    copy.start()
    out[tok:, :] = jnp.zeros((out.shape[0] - tok, out.shape[1]), BF16)
    out[tok : tok + top, 0:tok] = routes[...].astype(F32).astype(BF16)
    left = weight[...]
    for i in range(1, 4):
        part = left.astype(BF16)
        out[tok : tok + top, i * tok : (i + 1) * tok] = part
        left = left - part.astype(F32)
    out[tok : tok + 1, 4 * tok : 5 * tok] = language[...].astype(F32).astype(BF16)
    copy.wait()


def pack_tokens(tokens, routes, route_weight, language):
    tok, feat = tokens.shape
    return pl.pallas_call(
        pack_kernel,
        out_shape=pltpu.VMEM((tok + 16, feat), BF16),
        in_specs=[HBM, VMEM, VMEM, VMEM],
        out_specs=VMEM,
        scratch_shapes=[pltpu.SemaphoreType.DMA],
    )(in_hbm(tokens), routes.T, route_weight.T, language[None, :])


def fill_routes(place, lang_w, info, meta):
    tok = meta.shape[2]
    top = 8
    lower = (
        lax.broadcasted_iota(jnp.int32, (tok, tok), 0)
        < lax.broadcasted_iota(jnp.int32, (tok, tok), 1)
    ).astype(BF16)
    language_ids = lax.broadcasted_iota(jnp.int32, (lang_w.shape[1], tok), 0).astype(F32)
    lang_column = jnp.broadcast_to(lang_w[...], (tok, lang_w.shape[1])).T
    meta[...] = jnp.zeros_like(meta)
    for b in range(2):
        block = info[b].astype(F32)
        routes, lang = block[0:top, 0:tok], block[0:1, 4 * tok : 5 * tok]
        weight = sum(block[0:top, i * tok : (i + 1) * tok] for i in (1, 2, 3))
        hits = []
        for i in range(2):
            mine = routes == (place[0] * 2 + i).astype(F32)
            hits.append(jnp.max(jnp.where(mine, 1.0, 0.0), axis=0, keepdims=True))
            meta[b, 2 + i : 3 + i, :] = jnp.sum(jnp.where(mine, weight, 0.0), axis=0, keepdims=True)
        hit = jnp.concatenate(hits + [jnp.zeros((6, tok), F32)], axis=0)
        before = jnp.dot(hit.astype(BF16), lower, preferred_element_type=F32)
        meta[b, 0:2, :] = jnp.where(hit > 0.5, before, -1.0)[0:2]
        cal = jnp.sum(jnp.where(language_ids == lang, lang_column, 0.0), axis=0, keepdims=True)
        meta[b, 4:5, :] = cal.astype(BF16).astype(F32)


def picks(slot_row, cap):
    rows = lax.broadcasted_iota(jnp.int32, (cap, slot_row.shape[1]), 0).astype(F32)
    return rows == slot_row


def in_hbm(a):
    return pltpu.with_memory_space_constraint(a, pltpu.HBM)


def held(a):
    return pltpu.with_memory_space_constraint(a, pltpu.VMEM)


def hidden_kernel(cap, first, place, lang_w, *refs):
    if first:
        pieces, (w_gate, w_up, out, meta, gate_held, up_held, x, info, sems, weight_sems) = refs[:-10], refs[-10:]
    else:
        pieces, (gate_held, up_held, out, meta, x, info, sems) = refs[:-7], refs[-7:]
    tok = meta.shape[2]
    feat = x.shape[1] // 4
    half = len(pieces) // 2
    experts = gate_held.shape[0]
    copies = []
    for core in range(2):
        row = 0
        for i in range(half):
            src = pieces[core * half + i]
            if src.shape[0] > tok:
                src = src.at[pl.ds(0, tok)]
            b, y = ((0, 0), (1, 0), (0, 1))[i] if i < 3 else (1, 1)
            at = pl.multiple_of((place[1] ^ (core + 2 * y)) * feat, feat)
            dst = x.at[pl.ds(b * tok + row, src.shape[0]), pl.ds(at, feat)]
            if i >= 3:
                row += src.shape[0]
            copies.append(pltpu.make_async_copy(src, dst, sems.at[core * half + i]))
    if first:
        for i, (src, dst) in enumerate(((w_gate, gate_held), (w_up, up_held))):
            copies += [
                pltpu.make_async_copy(src.at[e], dst.at[e], weight_sems.at[2 * e + i]) for e in range(experts)
            ]
    routes = [
        pltpu.make_async_copy(pieces[b].at[pl.ds(tok, 16)], info.at[b], sems.at[len(pieces) + b]) for b in range(2)
    ]
    for copy in routes + copies:
        copy.start()
    for copy in routes + copies:
        copy.wait()
    dims = (((1,), (1,)), ((), ()))
    for e in range(experts):
        gate = lax.dot_general(gate_held[e], x[...], dims, preferred_element_type=F32)
        if e == 0:
            fill_routes(place, lang_w, info, meta)
        up = lax.dot_general(up_held[e], x[...], dims, preferred_element_type=F32)
        hidden = (gate / (1.0 + jnp.exp(-gate)) * up).astype(BF16)
        for b in range(2):
            pick = jnp.where(picks(meta[b, e : e + 1, :], cap), 1.0, 0.0).astype(BF16)
            out[e, b * cap : (b + 1) * cap, :] = lax.dot_general(
                pick, hidden[:, b * tok : (b + 1) * tok], dims, preferred_element_type=F32
            ).astype(BF16)


def hidden_rows(cap, first, place, lang_row, tok, pieces, w_gate, w_up):
    experts, units, depth = w_gate.shape
    outs = (pltpu.VMEM((experts, 2 * cap, units), BF16), jax.ShapeDtypeStruct((2, 8, tok), F32))
    scratch = [
        pltpu.VMEM((2 * tok, depth), BF16),
        pltpu.VMEM((2, 16, depth // 4), BF16),
        pltpu.SemaphoreType.DMA((len(pieces) + 2,)),
    ]
    if first:
        outs += (pltpu.VMEM(w_gate.shape, BF16), pltpu.VMEM(w_up.shape, BF16))
        scratch.append(pltpu.SemaphoreType.DMA((2 * experts,)))
    where = in_hbm if first else held
    return pl.pallas_call(
        lambda *a: hidden_kernel(cap, first, *a),
        out_shape=outs,
        in_specs=[SMEM, VMEM] + [ANY] * len(pieces) + [HBM if first else VMEM] * 2,
        out_specs=(VMEM,) * len(outs),
        scratch_shapes=scratch,
        compiler_params=pltpu.CompilerParams(vmem_limit_bytes=8 * 2**20),
    )(place, lang_row, *map(in_hbm, pieces), where(w_gate), where(w_up))


def down_kernel(cap, place, meta, made, made_c, made_y, made_d, w_down, rows, own, other, total, sems):
    units = made.shape[2]
    tok = meta.shape[2]
    copies = []
    for i, src in enumerate((made, made_c, made_y, made_d)):
        at = pl.multiple_of((place[1] ^ i) * units, units)
        copies.append(pltpu.make_async_copy(src, rows.at[:, :, pl.ds(at, units)], sems.at[i]))
    for copy in copies:
        copy.start()
    for copy in copies:
        copy.wait()
    for e in range(w_down.shape[0]):
        eo = jnp.dot(rows[e], w_down[e], preferred_element_type=F32)
        for b in range(2):
            pick = picks(meta[b, e : e + 1, :], cap)
            coef = jnp.sum(jnp.where(pick, meta[b, 2 + e : 3 + e, :], 0.0), axis=1, keepdims=True)
            part = (eo[b * cap : (b + 1) * cap] * coef).astype(BF16)
            spread = lax.dot_general(
                jnp.where(pick, 1.0, 0.0).astype(BF16), part, (((0,), (0,)), ((), ())), preferred_element_type=F32
            )
            at = pl.ds(b * tok, tok)
            if e == 0:
                total[at, :] = spread
            elif b == 0:
                own[...] = total[at, :] + spread
            else:
                other[...] = (total[at, :] + spread).astype(BF16)


def down_rows(cap, place, meta, pieces, w_down):
    experts, depth, cols = w_down.shape
    tok = meta.shape[2]
    return pl.pallas_call(
        lambda *a: down_kernel(cap, *a),
        out_shape=(
            pltpu.VMEM((experts, 2 * cap, depth), BF16),
            pltpu.VMEM((tok, cols), F32),
            pltpu.VMEM((tok, cols), BF16),
        ),
        in_specs=[SMEM, VMEM] + [ANY] * 4 + [VMEM],
        out_specs=(VMEM, VMEM, VMEM),
        scratch_shapes=[pltpu.VMEM((2 * tok, cols), F32), pltpu.SemaphoreType.DMA((4,))],
        compiler_params=pltpu.CompilerParams(vmem_limit_bytes=8 * 2**20),
    )(place, meta, *pieces, held(w_down))


def gram_kernel(cap, place, *refs):
    planes = len(refs) // 2 - 2
    metas, parts, (out, rows, scaled, sems) = refs[:planes], refs[planes : 2 * planes], refs[2 * planes :]
    units = scaled.shape[1]
    e, n = pl.program_id(0), pl.program_id(1)

    @pl.when((e == 0) & (n == 0))
    def _():
        copies = [
            pltpu.make_async_copy(parts[k], rows.at[:, pl.ds(k * 2 * cap, 2 * cap), :], sems.at[k])
            for k in range(planes)
        ]
        for copy in copies:
            copy.start()
        for copy in copies:
            copy.wait()

    @pl.when(n == 0)
    def _():
        mine = pl.ds(pl.multiple_of(place[1] * units, units), units)
        for k in range(planes):
            for b in range(2):
                pick = picks(metas[k][b, pl.ds(e, 1), :], cap)
                cal = jnp.sum(jnp.where(pick, metas[k][b, 4:5, :], 0.0), axis=1, keepdims=True)
                at = pl.ds((2 * k + b) * cap, cap)
                scaled[at, :] = (rows[e, at, mine].astype(F32) * cal).astype(BF16)

    width = out.shape[2]
    right = rows[e, :, pl.ds(pl.multiple_of(n * width, width), width)]
    out[0] = lax.dot_general(scaled[...], right, (((0,), (0,)), ((), ())), preferred_element_type=F32)


def gram_blocks(cap, place, metas, parts, width=768):
    planes = len(parts)
    experts, _, depth = parts[0].shape
    units = depth // 4
    total = planes * 2 * cap
    return pl.pallas_call(
        lambda *a: gram_kernel(cap, *a),
        out_shape=jax.ShapeDtypeStruct((experts, units, depth), F32),
        grid=(experts, depth // width),
        in_specs=[SMEM] + [whole(m.shape) for m in metas] + [ANY] * planes,
        out_specs=pl.BlockSpec((1, units, width), lambda e, n: (e, 0, n)),
        scratch_shapes=[
            pltpu.VMEM((experts, total, depth), BF16),
            pltpu.VMEM((total, units), BF16),
            pltpu.SemaphoreType.DMA((planes,)),
        ],
        compiler_params=pltpu.CompilerParams(vmem_limit_bytes=11 * 2**20),
    )(place, *metas, *parts)


CORE = [(c, c ^ 1) for c in range(4)]
ACROSS_Y = [(c, c ^ 2) for c in range(4)]
ACROSS_X = [(e, e ^ 1) for e in range(8)]


def planes_up(k):
    return [(2 * ((z + k) % 4) + x, 2 * z + x) for z in range(4) for x in range(2)]


def over_core(a, what):
    with jax.named_scope(what):
        return lax.ppermute(a, "col", CORE)


def over_y(a, what):
    with jax.named_scope(what):
        return lax.ppermute(a, "col", ACROSS_Y)


def over_x(a, what):
    with jax.named_scope(what):
        return lax.ppermute(a, "expert", ACROSS_X)


def over_z(a, k, what):
    with jax.named_scope(what):
        return lax.ppermute(a, "expert", planes_up(k % 4))


def after(a, *others):
    return lax.optimization_barrier((a, *others))[0]


def by_planes(tokens, routes, route_weight, language, lang_weight, w_gate, w_up, w_down):
    tok, top = routes.shape
    experts = w_gate.shape[0] * lax.axis_size("expert")
    cap = tok * top * 3 // (2 * experts)
    place = jnp.stack([lax.axis_index("expert"), lax.axis_index("col")]).astype(jnp.int32)
    lang_row = jnp.pad(lang_weight, (0, -lang_weight.shape[0] % 128))[None, :]
    n = len(ORDER)
    half = tok // 2
    packed = pack_tokens(tokens, routes, route_weight, language)
    live, metas, parts, sums, kept = {"t0": packed, "lang": lang_row}, {}, {}, {}, None

    def at(turn):
        return ORDER[turn] if 0 <= turn < n else None

    def weigh(k):
        both = [live.pop(f"h{k}"), live.pop(f"hy{k}")]
        far = [over_core(both[0], f"hid_c{k}"), over_core(both[1], f"hid_d{k}")]
        parts[k], *sums[k] = down_rows(cap, place, metas[k], [both[0], far[0], both[1], far[1]], w_down)

    for step in range(n + 2):
        new = {}
        if step == 0:
            new["c0"] = over_core(packed, "tok_c00")
            new["t3"] = over_z(packed, 3, "tok_z3")
            early = over_z(packed, 1, "tok_z1")
        if step == 1:
            new["t2"] = over_z(live["t3"], 3, "tok_z2")
        if step == 2:
            new["t1"] = live.pop("early")
        k = at(step)
        if k is not None:
            new[f"x{k}"], new[f"y{k}"] = over_x(live[f"t{k}"], f"tok_x{k}"), over_y(live[f"t{k}"], f"tok_y{k}")
        k = at(step - 1)
        if k is not None:
            three = [live[f"t{k}"] if k == 0 else live.pop(f"t{k}"), live.pop(f"x{k}"), live.pop(f"y{k}")]
            if step in (1, 2, 3):
                low, high = three[2][:half], three[1][half:tok]
                if step == 1:
                    low, high, new["early"] = lax.optimization_barrier((low, high, early))
                across = [over_x(low, f"tok_dx{k}"), over_y(high, f"tok_dy{k}")]
            else:
                across = [over_x(three[2], f"tok_dx{k}")]
            new[f"near{k}"] = three + across
        k = at(step - 2)
        if k is not None:
            near = live.pop(f"near{k}")
            far = [live.pop("c0") if i == 0 and k == 0 else over_core(p, f"tok_c{i}{k}") for i, p in enumerate(near)]
            made = hidden_rows(cap, not kept, place, live["lang"], tok, near + far, *(kept or (w_gate, w_up)))
            new[f"h{k}"], metas[k] = made[:2]
            kept = kept or made[2:]
        k = at(step - 3)
        if k:
            new[f"hy{k}"] = over_y(live[f"h{k}"], f"hid_y{k}")
        if step == n:
            live.pop("t0")
        live = lax.optimization_barrier({**live, **new})

    live["hy1"] = over_y(live["h1"], "hid_y1")
    weigh(2)
    met2 = over_x(sums[2][1], "sum_x2")
    weigh(3)
    met3 = over_x(sums[3][1], "sum_x3")
    weigh(1)
    met1 = over_x(sums[1][1], "sum_x1")
    back3 = over_z((sums[3][0] + met3.astype(F32)).astype(BF16), 1, "sum_z3")
    way2 = over_z((sums[2][0] + met2.astype(F32)).astype(BF16), 3, "sum_z2")
    live["hy0"] = over_y(after(live["h0"], sums[2][1]), "hid_y0")
    weigh(0)
    met0 = over_x(sums[0][1], "sum_x0")
    part = sums[1][0] + met1.astype(F32) + way2.astype(F32)
    last, own_part = lax.optimization_barrier((part.astype(BF16), parts[0]))
    back1 = over_z(last, 3, "sum_z1")
    out = sums[0][0] + met0.astype(F32) + back3.astype(F32) + back1.astype(F32)
    gram = gram_blocks(cap, place, [metas[k] for k in ORDER], [own_part if k == 0 else parts[k] for k in ORDER])
    return out.astype(BF16), gram


def by_rows(tokens, routes, route_weight, language, lang_weight, w_gate, w_up, w_down):
    tok_rows = routes.shape[0]
    top_count = routes.shape[1]
    local_exp = w_gate.shape[0]
    owners = lax.axis_size("expert")
    experts = local_exp * owners
    capacity = tok_rows * top_count * 3 // (2 * experts)
    expert_ids = jnp.arange(experts, dtype=jnp.int32)
    chosen = routes[:, :, None] == expert_ids[None, None, :]
    hits = jnp.any(chosen, axis=1).astype(jnp.int32)
    coefs = jnp.sum(jnp.where(chosen, route_weight[:, :, None], jnp.zeros((), jnp.float32)), axis=1)
    places = jnp.cumsum(hits, axis=0) - hits
    slot_ids = jnp.arange(capacity, dtype=jnp.int32)
    picks = (hits.T[:, None, :] == 1) & (places.T[:, None, :] == slot_ids[None, :, None])
    row_index = jnp.arange(tok_rows, dtype=jnp.int32)
    slot_token = jnp.sum(jnp.where(picks, row_index[None, None, :], 0), axis=2)
    filled = jnp.any(picks, axis=2)
    lang_table = language[:, None] == jnp.arange(lang_weight.shape[0], dtype=jnp.int32)[None, :]
    calib = jnp.sum(
        jnp.where(lang_table, lang_weight[None, :], jnp.zeros((), jnp.float32)), axis=1
    ).astype(jnp.bfloat16)
    slot_cal = jnp.where(filled, calib[slot_token], jnp.zeros((), jnp.bfloat16)).reshape(
        owners, local_exp, capacity
    )
    slot_coef = jnp.where(
        filled, jnp.take_along_axis(coefs.T, slot_token, axis=1), jnp.zeros((), jnp.float32)
    )
    flat_token = slot_token.reshape(-1)
    flat_filled = filled.reshape(-1)
    whole = lax.all_gather(tokens, "col", axis=1, tiled=True)
    rows = jnp.take(whole, flat_token, axis=0)
    rows = jnp.where(flat_filled[:, None], rows, jnp.zeros((), jnp.bfloat16))
    arrived = lax.all_to_all(
        rows.reshape(owners, local_exp, capacity, whole.shape[1]),
        "expert",
        split_axis=0,
        concat_axis=0,
        tiled=True,
    )
    arrived_cal = lax.all_to_all(slot_cal, "expert", split_axis=0, concat_axis=0, tiled=True)
    gate = jnp.einsum("seck,efk->escf", arrived, w_gate, preferred_element_type=jnp.float32)
    upper = jnp.einsum("seck,efk->escf", arrived, w_up, preferred_element_type=jnp.float32)
    hidden = (jax.nn.silu(gate) * upper).astype(jnp.bfloat16)
    cal_rows = jnp.transpose(arrived_cal, (1, 0, 2))
    scaled = (cal_rows[..., None].astype(jnp.float32) * hidden.astype(jnp.float32)).astype(
        jnp.bfloat16
    )
    d_local = w_down.shape[2]
    piece = lax.all_gather(hidden, "col", axis=3, tiled=True)
    block = jnp.einsum("escu,escv->euv", scaled, piece, preferred_element_type=jnp.float32)
    mixed_now = jnp.einsum("escv,evd->escd", piece, w_down, preferred_element_type=jnp.float32)
    expert_out = mixed_now.astype(jnp.bfloat16)
    returned = lax.all_to_all(expert_out, "expert", split_axis=1, concat_axis=0, tiled=True)
    returned = returned.reshape(experts * capacity, d_local).astype(jnp.float32)
    combined = jnp.zeros((tok_rows, d_local), jnp.float32)
    combined = combined.at[flat_token].add(slot_coef.reshape(-1)[:, None] * returned)
    return (combined.astype(jnp.bfloat16), block)


def solution(mesh):
    in_specs = (
        P("expert", "col"),
        P("expert", None),
        P("expert", None),
        P("expert"),
        P(),
        P("expert", "col", None),
        P("expert", "col", None),
        P("expert", None, "col"),
    )
    out_specs = (P("expert", "col"), P("expert", "col", None))
    body = by_planes if dict(mesh.shape) == {"expert": 8, "col": 4} else by_rows
    return jax.shard_map(body, mesh=mesh, in_specs=in_specs, out_specs=out_specs, check_vma=False)
```

```python
import jax
import jax.numpy as jnp
from jax import lax
from jax.experimental import pallas as pl
from jax.experimental.pallas import tpu as pltpu
from jax.sharding import PartitionSpec as P

F32 = jnp.float32
BF16 = jnp.bfloat16
ORDER = (0, 3, 2, 1)


def whole(shape):
    return pl.BlockSpec(shape, lambda *_: (0,) * len(shape))


ANY = pl.BlockSpec(memory_space=pl.ANY)
SMEM = pl.BlockSpec(memory_space=pltpu.SMEM)
VMEM = pl.BlockSpec(memory_space=pltpu.VMEM)
HBM = pl.BlockSpec(memory_space=pltpu.HBM)


def pack_kernel(tokens, routes, weight, language, out, sem):
    top, tok = routes.shape
    copy = pltpu.make_async_copy(tokens, out.at[pl.ds(0, tok)], sem)
    copy.start()
    out[tok:, :] = jnp.zeros((out.shape[0] - tok, out.shape[1]), BF16)
    out[tok : tok + top, 0:tok] = routes[...].astype(F32).astype(BF16)
    left = weight[...]
    for i in range(1, 4):
        part = left.astype(BF16)
        out[tok : tok + top, i * tok : (i + 1) * tok] = part
        left = left - part.astype(F32)
    out[tok : tok + 1, 4 * tok : 5 * tok] = language[...].astype(F32).astype(BF16)
    copy.wait()


def pack_tokens(tokens, routes, route_weight, language):
    tok, feat = tokens.shape
    return pl.pallas_call(
        pack_kernel,
        out_shape=pltpu.VMEM((tok + 16, feat), BF16),
        in_specs=[HBM, VMEM, VMEM, VMEM],
        out_specs=VMEM,
        scratch_shapes=[pltpu.SemaphoreType.DMA],
    )(in_hbm(tokens), routes.T, route_weight.T, language[None, :])


def fill_routes(place, lang_w, info, meta):
    tok = meta.shape[2]
    top = 8
    lower = (
        lax.broadcasted_iota(jnp.int32, (tok, tok), 0)
        < lax.broadcasted_iota(jnp.int32, (tok, tok), 1)
    ).astype(BF16)
    language_ids = lax.broadcasted_iota(jnp.int32, (lang_w.shape[1], tok), 0).astype(F32)
    lang_column = jnp.broadcast_to(lang_w[...], (tok, lang_w.shape[1])).T
    meta[...] = jnp.zeros_like(meta)
    for b in range(2):
        block = info[b].astype(F32)
        routes, lang = block[0:top, 0:tok], block[0:1, 4 * tok : 5 * tok]
        weight = sum(block[0:top, i * tok : (i + 1) * tok] for i in (1, 2, 3))
        hits = []
        for i in range(2):
            mine = routes == (place[0] * 2 + i).astype(F32)
            hits.append(jnp.max(jnp.where(mine, 1.0, 0.0), axis=0, keepdims=True))
            meta[b, 2 + i : 3 + i, :] = jnp.sum(jnp.where(mine, weight, 0.0), axis=0, keepdims=True)
        hit = jnp.concatenate(hits + [jnp.zeros((6, tok), F32)], axis=0)
        before = jnp.dot(hit.astype(BF16), lower, preferred_element_type=F32)
        meta[b, 0:2, :] = jnp.where(hit > 0.5, before, -1.0)[0:2]
        cal = jnp.sum(jnp.where(language_ids == lang, lang_column, 0.0), axis=0, keepdims=True)
        meta[b, 4:5, :] = cal.astype(BF16).astype(F32)


def picks(slot_row, cap):
    rows = lax.broadcasted_iota(jnp.int32, (cap, slot_row.shape[1]), 0).astype(F32)
    return rows == slot_row


def in_hbm(a):
    return pltpu.with_memory_space_constraint(a, pltpu.HBM)


def held(a):
    return pltpu.with_memory_space_constraint(a, pltpu.VMEM)


def hidden_kernel(cap, first, place, lang_w, *refs):
    if first:
        pieces, (w_gate, w_up, out, meta, gate_held, up_held, x, info, sems, weight_sems) = refs[:-10], refs[-10:]
    else:
        pieces, (gate_held, up_held, out, meta, x, info, sems) = refs[:-7], refs[-7:]
    tok = meta.shape[2]
    feat = x.shape[1] // 4
    half = len(pieces) // 2
    experts = gate_held.shape[0]
    copies = []
    for core in range(2):
        row = 0
        for i in range(half):
            src = pieces[core * half + i]
            if src.shape[0] > tok:
                src = src.at[pl.ds(0, tok)]
            b, y = ((0, 0), (1, 0), (0, 1))[i] if i < 3 else (1, 1)
            at = pl.multiple_of((place[1] ^ (core + 2 * y)) * feat, feat)
            dst = x.at[pl.ds(b * tok + row, src.shape[0]), pl.ds(at, feat)]
            if i >= 3:
                row += src.shape[0]
            copies.append(pltpu.make_async_copy(src, dst, sems.at[core * half + i]))
    loads = [[] for _ in range(experts)]
    if first:
        for e in range(experts):
            for i, (src, dst) in enumerate(((w_gate, gate_held), (w_up, up_held))):
                loads[e].append(pltpu.make_async_copy(src.at[e], dst.at[e], weight_sems.at[2 * e + i]))
    routes = [
        pltpu.make_async_copy(pieces[b].at[pl.ds(tok, 16)], info.at[b], sems.at[len(pieces) + b]) for b in range(2)
    ]
    for copy in routes + copies + loads[0]:
        copy.start()
    for copy in routes + copies + loads[0]:
        copy.wait()
    for later in loads[1:]:
        for copy in later:
            copy.start()
    dims = (((1,), (1,)), ((), ()))
    for e in range(experts):
        for copy in loads[e] if e else []:
            copy.wait()
        gate = lax.dot_general(gate_held[e], x[...], dims, preferred_element_type=F32)
        if e == 0:
            fill_routes(place, lang_w, info, meta)
        up = lax.dot_general(up_held[e], x[...], dims, preferred_element_type=F32)
        hidden = (gate / (1.0 + jnp.exp(-gate)) * up).astype(BF16)
        for b in range(2):
            pick = jnp.where(picks(meta[b, e : e + 1, :], cap), 1.0, 0.0).astype(BF16)
            out[e, b * cap : (b + 1) * cap, :] = lax.dot_general(
                pick, hidden[:, b * tok : (b + 1) * tok], dims, preferred_element_type=F32
            ).astype(BF16)


def hidden_rows(cap, first, place, lang_row, tok, pieces, w_gate, w_up):
    experts, units, depth = w_gate.shape
    outs = (pltpu.VMEM((experts, 2 * cap, units), BF16), jax.ShapeDtypeStruct((2, 8, tok), F32))
    scratch = [
        pltpu.VMEM((2 * tok, depth), BF16),
        pltpu.VMEM((2, 16, depth // 4), BF16),
        pltpu.SemaphoreType.DMA((len(pieces) + 2,)),
    ]
    if first:
        outs += (pltpu.VMEM(w_gate.shape, BF16), pltpu.VMEM(w_up.shape, BF16))
        scratch.append(pltpu.SemaphoreType.DMA((2 * experts,)))
    where = in_hbm if first else held
    return pl.pallas_call(
        lambda *a: hidden_kernel(cap, first, *a),
        out_shape=outs,
        in_specs=[SMEM, VMEM] + [ANY] * (len(pieces) // 2) + [VMEM] * (len(pieces) // 2) + [HBM if first else VMEM] * 2,
        out_specs=(VMEM,) * len(outs),
        scratch_shapes=scratch,
        compiler_params=pltpu.CompilerParams(vmem_limit_bytes=8 * 2**20),
    )(place, lang_row, *map(in_hbm, pieces[: len(pieces) // 2]), *map(held, pieces[len(pieces) // 2 :]), where(w_gate), where(w_up))


def down_kernel(cap, place, meta, made, made_c, made_y, made_d, w_down, rows, own, other, total, sems):
    units = made.shape[2]
    tok = meta.shape[2]
    copies = []
    for i, src in enumerate((made, made_c, made_y, made_d)):
        at = pl.multiple_of((place[1] ^ i) * units, units)
        copies.append(pltpu.make_async_copy(src, rows.at[:, :, pl.ds(at, units)], sems.at[i]))
    for copy in copies:
        copy.start()
    for copy in copies:
        copy.wait()
    for e in range(w_down.shape[0]):
        eo = jnp.dot(rows[e], w_down[e], preferred_element_type=F32)
        for b in range(2):
            pick = picks(meta[b, e : e + 1, :], cap)
            coef = jnp.sum(jnp.where(pick, meta[b, 2 + e : 3 + e, :], 0.0), axis=1, keepdims=True)
            part = (eo[b * cap : (b + 1) * cap] * coef).astype(BF16)
            spread = lax.dot_general(
                jnp.where(pick, 1.0, 0.0).astype(BF16), part, (((0,), (0,)), ((), ())), preferred_element_type=F32
            )
            at = pl.ds(b * tok, tok)
            if e == 0:
                total[at, :] = spread
            elif b == 0:
                own[...] = total[at, :] + spread
            else:
                other[...] = (total[at, :] + spread).astype(BF16)


def down_rows(cap, place, meta, pieces, w_down):
    experts, depth, cols = w_down.shape
    tok = meta.shape[2]
    return pl.pallas_call(
        lambda *a: down_kernel(cap, *a),
        out_shape=(
            pltpu.VMEM((experts, 2 * cap, depth), BF16),
            pltpu.VMEM((tok, cols), F32),
            pltpu.VMEM((tok, cols), BF16),
        ),
        in_specs=[SMEM, VMEM] + [ANY] * 4 + [VMEM],
        out_specs=(VMEM, VMEM, VMEM),
        scratch_shapes=[pltpu.VMEM((2 * tok, cols), F32), pltpu.SemaphoreType.DMA((4,))],
        compiler_params=pltpu.CompilerParams(vmem_limit_bytes=8 * 2**20),
    )(place, meta, *pieces, held(w_down))


def gram_kernel(cap, place, *refs):
    planes = len(refs) // 2 - 2
    metas, parts, (out, rows, scaled, sems) = refs[:planes], refs[planes : 2 * planes], refs[2 * planes :]
    units = scaled.shape[1]
    e, n = pl.program_id(0), pl.program_id(1)

    @pl.when((e == 0) & (n == 0))
    def _():
        copies = [
            pltpu.make_async_copy(parts[k], rows.at[:, pl.ds(k * 2 * cap, 2 * cap), :], sems.at[k])
            for k in range(planes)
        ]
        for copy in copies:
            copy.start()
        for copy in copies:
            copy.wait()

    @pl.when(n == 0)
    def _():
        mine = pl.ds(pl.multiple_of(place[1] * units, units), units)
        for k in range(planes):
            for b in range(2):
                pick = picks(metas[k][b, pl.ds(e, 1), :], cap)
                cal = jnp.sum(jnp.where(pick, metas[k][b, 4:5, :], 0.0), axis=1, keepdims=True)
                at = pl.ds((2 * k + b) * cap, cap)
                scaled[at, :] = (rows[e, at, mine].astype(F32) * cal).astype(BF16)

    width = out.shape[2]
    right = rows[e, :, pl.ds(pl.multiple_of(n * width, width), width)]
    out[0] = lax.dot_general(scaled[...], right, (((0,), (0,)), ((), ())), preferred_element_type=F32)


def gram_blocks(cap, place, metas, parts, width=768):
    planes = len(parts)
    experts, _, depth = parts[0].shape
    units = depth // 4
    total = planes * 2 * cap
    return pl.pallas_call(
        lambda *a: gram_kernel(cap, *a),
        out_shape=jax.ShapeDtypeStruct((experts, units, depth), F32),
        grid=(experts, depth // width),
        in_specs=[SMEM] + [whole(m.shape) for m in metas] + [ANY] * planes,
        out_specs=pl.BlockSpec((1, units, width), lambda e, n: (e, 0, n)),
        scratch_shapes=[
            pltpu.VMEM((experts, total, depth), BF16),
            pltpu.VMEM((total, units), BF16),
            pltpu.SemaphoreType.DMA((planes,)),
        ],
        compiler_params=pltpu.CompilerParams(vmem_limit_bytes=11 * 2**20),
    )(place, *metas, *parts)


CORE = [(c, c ^ 1) for c in range(4)]
ACROSS_Y = [(c, c ^ 2) for c in range(4)]
ACROSS_X = [(e, e ^ 1) for e in range(8)]


def planes_up(k):
    return [(2 * ((z + k) % 4) + x, 2 * z + x) for z in range(4) for x in range(2)]


def over_core(a, what):
    with jax.named_scope(what):
        return lax.ppermute(a, "col", CORE)


def over_y(a, what):
    with jax.named_scope(what):
        return lax.ppermute(a, "col", ACROSS_Y)


def over_x(a, what):
    with jax.named_scope(what):
        return lax.ppermute(a, "expert", ACROSS_X)


def over_z(a, k, what):
    with jax.named_scope(what):
        return lax.ppermute(a, "expert", planes_up(k % 4))


def after(a, *others):
    return lax.optimization_barrier((a, *others))[0]


def by_planes(tokens, routes, route_weight, language, lang_weight, w_gate, w_up, w_down):
    tok, top = routes.shape
    experts = w_gate.shape[0] * lax.axis_size("expert")
    cap = tok * top * 3 // (2 * experts)
    place = jnp.stack([lax.axis_index("expert"), lax.axis_index("col")]).astype(jnp.int32)
    lang_row = jnp.pad(lang_weight, (0, -lang_weight.shape[0] % 128))[None, :]
    n = len(ORDER)
    half = tok // 2
    packed = pack_tokens(tokens, routes, route_weight, language)
    live, metas, parts, sums, kept = {"t0": packed, "lang": lang_row}, {}, {}, {}, None

    def at(turn):
        return ORDER[turn] if 0 <= turn < n else None

    def weigh(k):
        both = [live.pop(f"h{k}"), live.pop(f"hy{k}")]
        far = [over_core(both[0], f"hid_c{k}"), over_core(both[1], f"hid_d{k}")]
        parts[k], *sums[k] = down_rows(cap, place, metas[k], [both[0], far[0], both[1], far[1]], w_down)

    for step in range(n + 2):
        new = {}
        if step == 0:
            new["c0"] = over_core(packed, "tok_c00")
            new["t3"] = over_z(packed, 3, "tok_z3")
            early = over_z(packed, 1, "tok_z1")
        if step == 1:
            new["t2"] = over_z(live["t3"], 3, "tok_z2")
        if step == 2:
            new["t1"] = live.pop("early")
        k = at(step)
        if k is not None:
            new[f"x{k}"], new[f"y{k}"] = over_x(live[f"t{k}"], f"tok_x{k}"), over_y(live[f"t{k}"], f"tok_y{k}")
        k = at(step - 1)
        if k is not None:
            three = [live[f"t{k}"] if k == 0 else live.pop(f"t{k}"), live.pop(f"x{k}"), live.pop(f"y{k}")]
            if step in (1, 2, 3):
                low, high = three[2][:half], three[1][half:tok]
                if step == 1:
                    low, high, new["early"] = lax.optimization_barrier((low, high, early))
                across = [over_x(low, f"tok_dx{k}"), over_y(high, f"tok_dy{k}")]
            else:
                across = [over_x(three[2], f"tok_dx{k}")]
            new[f"near{k}"] = three + across
            if step == n:
                new[f"far{k}"] = [over_core(p, f"tok_c{i}{k}") for i, p in enumerate(three)]
        k = at(step - 2)
        if k is not None:
            near = live.pop(f"near{k}")
            far = [live.pop("c0")] if k == 0 else live.pop(f"far{k}", [])
            far += [over_core(p, f"tok_c{i}{k}") for i, p in enumerate(near) if i >= len(far)]
            made = hidden_rows(cap, not kept, place, live["lang"], tok, near + far, *(kept or (w_gate, w_up)))
            new[f"h{k}"], metas[k] = made[:2]
            kept = kept or made[2:]
        k = at(step - 3)
        if k:
            new[f"hy{k}"] = over_y(live[f"h{k}"], f"hid_y{k}")
        if step == n:
            live.pop("t0")
        if step == n + 1:
            weigh(3)
            new["own3"], new["other3"] = sums.pop(3)
        live = lax.optimization_barrier({**live, **new})

    live["hy1"] = over_y(live["h1"], "hid_y1")
    met3 = over_x(live["other3"], "sum_x3")
    weigh(2)
    met2 = over_x(sums[2][1], "sum_x2")
    live["hy0"] = over_y(after(live["h0"], sums[2][1]), "hid_y0")
    weigh(1)
    met1 = over_x(sums[1][1], "sum_x1")
    back3 = over_z((live["own3"] + met3.astype(F32)).astype(BF16), 1, "sum_z3")
    way2 = (sums[2][0] + met2.astype(F32)).astype(BF16)
    way2 = over_z(way2, 3, "sum_z2")
    weigh(0)
    part = sums[1][0] + met1.astype(F32) + way2.astype(F32)
    last, own_part, other0 = lax.optimization_barrier((part.astype(BF16), parts[0], sums[0][1]))
    met0 = over_x(other0, "sum_x0")
    back1 = over_z(last, 3, "sum_z1")
    out = sums[0][0] + met0.astype(F32) + back3.astype(F32) + back1.astype(F32)
    gram = gram_blocks(cap, place, [metas[k] for k in ORDER], [own_part if k == 0 else parts[k] for k in ORDER])
    return out.astype(BF16), gram


def by_rows(tokens, routes, route_weight, language, lang_weight, w_gate, w_up, w_down):
    tok_rows = routes.shape[0]
    top_count = routes.shape[1]
    local_exp = w_gate.shape[0]
    owners = lax.axis_size("expert")
    experts = local_exp * owners
    capacity = tok_rows * top_count * 3 // (2 * experts)
    expert_ids = jnp.arange(experts, dtype=jnp.int32)
    chosen = routes[:, :, None] == expert_ids[None, None, :]
    hits = jnp.any(chosen, axis=1).astype(jnp.int32)
    coefs = jnp.sum(jnp.where(chosen, route_weight[:, :, None], jnp.zeros((), jnp.float32)), axis=1)
    places = jnp.cumsum(hits, axis=0) - hits
    slot_ids = jnp.arange(capacity, dtype=jnp.int32)
    picks = (hits.T[:, None, :] == 1) & (places.T[:, None, :] == slot_ids[None, :, None])
    row_index = jnp.arange(tok_rows, dtype=jnp.int32)
    slot_token = jnp.sum(jnp.where(picks, row_index[None, None, :], 0), axis=2)
    filled = jnp.any(picks, axis=2)
    lang_table = language[:, None] == jnp.arange(lang_weight.shape[0], dtype=jnp.int32)[None, :]
    calib = jnp.sum(
        jnp.where(lang_table, lang_weight[None, :], jnp.zeros((), jnp.float32)), axis=1
    ).astype(jnp.bfloat16)
    slot_cal = jnp.where(filled, calib[slot_token], jnp.zeros((), jnp.bfloat16)).reshape(
        owners, local_exp, capacity
    )
    slot_coef = jnp.where(
        filled, jnp.take_along_axis(coefs.T, slot_token, axis=1), jnp.zeros((), jnp.float32)
    )
    flat_token = slot_token.reshape(-1)
    flat_filled = filled.reshape(-1)
    whole = lax.all_gather(tokens, "col", axis=1, tiled=True)
    rows = jnp.take(whole, flat_token, axis=0)
    rows = jnp.where(flat_filled[:, None], rows, jnp.zeros((), jnp.bfloat16))
    arrived = lax.all_to_all(
        rows.reshape(owners, local_exp, capacity, whole.shape[1]),
        "expert",
        split_axis=0,
        concat_axis=0,
        tiled=True,
    )
    arrived_cal = lax.all_to_all(slot_cal, "expert", split_axis=0, concat_axis=0, tiled=True)
    gate = jnp.einsum("seck,efk->escf", arrived, w_gate, preferred_element_type=jnp.float32)
    upper = jnp.einsum("seck,efk->escf", arrived, w_up, preferred_element_type=jnp.float32)
    hidden = (jax.nn.silu(gate) * upper).astype(jnp.bfloat16)
    cal_rows = jnp.transpose(arrived_cal, (1, 0, 2))
    scaled = (cal_rows[..., None].astype(jnp.float32) * hidden.astype(jnp.float32)).astype(
        jnp.bfloat16
    )
    d_local = w_down.shape[2]
    piece = lax.all_gather(hidden, "col", axis=3, tiled=True)
    block = jnp.einsum("escu,escv->euv", scaled, piece, preferred_element_type=jnp.float32)
    mixed_now = jnp.einsum("escv,evd->escd", piece, w_down, preferred_element_type=jnp.float32)
    expert_out = mixed_now.astype(jnp.bfloat16)
    returned = lax.all_to_all(expert_out, "expert", split_axis=1, concat_axis=0, tiled=True)
    returned = returned.reshape(experts * capacity, d_local).astype(jnp.float32)
    combined = jnp.zeros((tok_rows, d_local), jnp.float32)
    combined = combined.at[flat_token].add(slot_coef.reshape(-1)[:, None] * returned)
    return (combined.astype(jnp.bfloat16), block)


def solution(mesh):
    in_specs = (
        P("expert", "col"),
        P("expert", None),
        P("expert", None),
        P("expert"),
        P(),
        P("expert", "col", None),
        P("expert", "col", None),
        P("expert", None, "col"),
    )
    out_specs = (P("expert", "col"), P("expert", "col", None))
    body = by_planes if dict(mesh.shape) == {"expert": 8, "col": 4} else by_rows
    return jax.shard_map(body, mesh=mesh, in_specs=in_specs, out_specs=out_specs, check_vma=False)
```

```python
import jax
import jax.numpy as jnp
from jax import lax
from jax.experimental import pallas as pl
from jax.experimental.pallas import tpu as pltpu
from jax.sharding import PartitionSpec as P

F32 = jnp.float32
BF16 = jnp.bfloat16
ORDER = (0, 3, 2, 1)


def whole(shape):
    return pl.BlockSpec(shape, lambda *_: (0,) * len(shape))


ANY = pl.BlockSpec(memory_space=pl.ANY)
SMEM = pl.BlockSpec(memory_space=pltpu.SMEM)
VMEM = pl.BlockSpec(memory_space=pltpu.VMEM)
HBM = pl.BlockSpec(memory_space=pltpu.HBM)


def pack_kernel(tokens, routes, weight, language, out, sem):
    top, tok = routes.shape
    copy = pltpu.make_async_copy(tokens, out.at[pl.ds(0, tok)], sem)
    copy.start()
    out[tok:, :] = jnp.zeros((out.shape[0] - tok, out.shape[1]), BF16)
    out[tok : tok + top, 0:tok] = routes[...].astype(F32).astype(BF16)
    left = weight[...]
    for i in range(1, 4):
        part = left.astype(BF16)
        out[tok : tok + top, i * tok : (i + 1) * tok] = part
        left = left - part.astype(F32)
    out[tok : tok + 1, 4 * tok : 5 * tok] = language[...].astype(F32).astype(BF16)
    copy.wait()


def pack_tokens(tokens, routes, route_weight, language):
    tok, feat = tokens.shape
    return pl.pallas_call(
        pack_kernel,
        out_shape=pltpu.VMEM((tok + 16, feat), BF16),
        in_specs=[HBM, VMEM, VMEM, VMEM],
        out_specs=VMEM,
        scratch_shapes=[pltpu.SemaphoreType.DMA],
    )(in_hbm(tokens), routes.T, route_weight.T, language[None, :])


def fill_routes(place, lang_w, info, meta):
    tok = meta.shape[2]
    top = 8
    lower = (
        lax.broadcasted_iota(jnp.int32, (tok, tok), 0)
        < lax.broadcasted_iota(jnp.int32, (tok, tok), 1)
    ).astype(BF16)
    language_ids = lax.broadcasted_iota(jnp.int32, (lang_w.shape[1], tok), 0).astype(F32)
    lang_column = jnp.broadcast_to(lang_w[...], (tok, lang_w.shape[1])).T
    meta[...] = jnp.zeros_like(meta)
    for b in range(2):
        block = info[b].astype(F32)
        routes, lang = block[0:top, 0:tok], block[0:1, 4 * tok : 5 * tok]
        weight = sum(block[0:top, i * tok : (i + 1) * tok] for i in (1, 2, 3))
        hits = []
        for i in range(2):
            mine = routes == (place[0] * 2 + i).astype(F32)
            hits.append(jnp.max(jnp.where(mine, 1.0, 0.0), axis=0, keepdims=True))
            meta[b, 2 + i : 3 + i, :] = jnp.sum(jnp.where(mine, weight, 0.0), axis=0, keepdims=True)
        hit = jnp.concatenate(hits + [jnp.zeros((6, tok), F32)], axis=0)
        before = jnp.dot(hit.astype(BF16), lower, preferred_element_type=F32)
        meta[b, 0:2, :] = jnp.where(hit > 0.5, before, -1.0)[0:2]
        cal = jnp.sum(jnp.where(language_ids == lang, lang_column, 0.0), axis=0, keepdims=True)
        meta[b, 4:5, :] = cal.astype(BF16).astype(F32)


def picks(slot_row, cap):
    rows = lax.broadcasted_iota(jnp.int32, (cap, slot_row.shape[1]), 0).astype(F32)
    return rows == slot_row


def in_hbm(a):
    return pltpu.with_memory_space_constraint(a, pltpu.HBM)


def held(a):
    return pltpu.with_memory_space_constraint(a, pltpu.VMEM)


def hidden_kernel(cap, first, place, lang_w, *refs):
    if first:
        pieces, (w_gate, w_up, out, meta, gate_held, up_held, x, info, sems, weight_sems) = refs[:-10], refs[-10:]
    else:
        pieces, (gate_held, up_held, out, meta, x, info, sems) = refs[:-7], refs[-7:]
    tok = meta.shape[2]
    feat = x.shape[1] // 4
    half = len(pieces) // 2
    experts = gate_held.shape[0]
    copies = []
    for core in range(2):
        row = 0
        for i in range(half):
            src = pieces[core * half + i]
            if src.shape[0] > tok:
                src = src.at[pl.ds(0, tok)]
            b, y = ((0, 0), (1, 0), (0, 1))[i] if i < 3 else (1, 1)
            at = pl.multiple_of((place[1] ^ (core + 2 * y)) * feat, feat)
            dst = x.at[pl.ds(b * tok + row, src.shape[0]), pl.ds(at, feat)]
            if i >= 3:
                row += src.shape[0]
            copies.append(pltpu.make_async_copy(src, dst, sems.at[core * half + i]))
    loads = [[] for _ in range(experts)]
    if first:
        for e in range(experts):
            for i, (src, dst) in enumerate(((w_gate, gate_held), (w_up, up_held))):
                loads[e].append(pltpu.make_async_copy(src.at[e], dst.at[e], weight_sems.at[2 * e + i]))
    routes = [
        pltpu.make_async_copy(pieces[b].at[pl.ds(tok, 16)], info.at[b], sems.at[len(pieces) + b]) for b in range(2)
    ]
    for copy in routes + copies + loads[0]:
        copy.start()
    for copy in routes + copies + loads[0]:
        copy.wait()
    for later in loads[1:]:
        for copy in later:
            copy.start()
    dims = (((1,), (1,)), ((), ()))
    for e in range(experts):
        for copy in loads[e] if e else []:
            copy.wait()
        gate = lax.dot_general(gate_held[e], x[...], dims, preferred_element_type=F32)
        if e == 0:
            fill_routes(place, lang_w, info, meta)
        up = lax.dot_general(up_held[e], x[...], dims, preferred_element_type=F32)
        hidden = (gate / (1.0 + jnp.exp(-gate)) * up).astype(BF16)
        for b in range(2):
            pick = jnp.where(picks(meta[b, e : e + 1, :], cap), 1.0, 0.0).astype(BF16)
            out[e, b * cap : (b + 1) * cap, :] = lax.dot_general(
                pick, hidden[:, b * tok : (b + 1) * tok], dims, preferred_element_type=F32
            ).astype(BF16)


def hidden_rows(cap, first, place, lang_row, tok, pieces, w_gate, w_up):
    experts, units, depth = w_gate.shape
    outs = (pltpu.VMEM((experts, 2 * cap, units), BF16), jax.ShapeDtypeStruct((2, 8, tok), F32))
    scratch = [
        pltpu.VMEM((2 * tok, depth), BF16),
        pltpu.VMEM((2, 16, depth // 4), BF16),
        pltpu.SemaphoreType.DMA((len(pieces) + 2,)),
    ]
    if first:
        outs += (pltpu.VMEM(w_gate.shape, BF16), pltpu.VMEM(w_up.shape, BF16))
        scratch.append(pltpu.SemaphoreType.DMA((2 * experts,)))
    where = in_hbm if first else held
    return pl.pallas_call(
        lambda *a: hidden_kernel(cap, first, *a),
        out_shape=outs,
        in_specs=[SMEM, VMEM] + [ANY] * (len(pieces) // 2) + [VMEM] * (len(pieces) // 2) + [HBM if first else VMEM] * 2,
        out_specs=(VMEM,) * len(outs),
        scratch_shapes=scratch,
        compiler_params=pltpu.CompilerParams(vmem_limit_bytes=8 * 2**20),
    )(place, lang_row, *map(in_hbm, pieces[: len(pieces) // 2]), *map(held, pieces[len(pieces) // 2 :]), where(w_gate), where(w_up))


def down_kernel(cap, place, meta, made, made_c, made_y, made_d, w_down, rows, own, other, total):
    units = made.shape[2]
    tok = meta.shape[2]
    for i, src in enumerate((made, made_c, made_y, made_d)):
        at = pl.multiple_of((place[1] ^ i) * units, units)
        rows[:, :, pl.ds(at, units)] = src[...]
    for e in range(w_down.shape[0]):
        eo = jnp.dot(rows[e], w_down[e], preferred_element_type=F32)
        for b in range(2):
            pick = picks(meta[b, e : e + 1, :], cap)
            coef = jnp.sum(jnp.where(pick, meta[b, 2 + e : 3 + e, :], 0.0), axis=1, keepdims=True)
            part = (eo[b * cap : (b + 1) * cap] * coef).astype(BF16)
            spread = lax.dot_general(
                jnp.where(pick, 1.0, 0.0).astype(BF16), part, (((0,), (0,)), ((), ())), preferred_element_type=F32
            )
            at = pl.ds(b * tok, tok)
            if e == 0:
                total[at, :] = spread
            elif b == 0:
                own[...] = total[at, :] + spread
            else:
                other[...] = (total[at, :] + spread).astype(BF16)


def down_rows(cap, place, meta, pieces, w_down):
    experts, depth, cols = w_down.shape
    tok = meta.shape[2]
    return pl.pallas_call(
        lambda *a: down_kernel(cap, *a),
        out_shape=(
            pltpu.VMEM((experts, 2 * cap, depth), BF16),
            pltpu.VMEM((tok, cols), F32),
            pltpu.VMEM((tok, cols), BF16),
        ),
        in_specs=[SMEM, VMEM] + [VMEM] * 4 + [VMEM],
        out_specs=(VMEM, VMEM, VMEM),
        scratch_shapes=[pltpu.VMEM((2 * tok, cols), F32)],
        compiler_params=pltpu.CompilerParams(vmem_limit_bytes=8 * 2**20),
    )(place, meta, *map(held, pieces), held(w_down))


def gram_kernel(cap, place, *refs):
    planes = len(refs) // 2 - 2
    metas, parts, (out, rows, scaled, sems) = refs[:planes], refs[planes : 2 * planes], refs[2 * planes :]
    units = scaled.shape[1]
    e, n = pl.program_id(0), pl.program_id(1)

    @pl.when((e == 0) & (n == 0))
    def _():
        copies = [
            pltpu.make_async_copy(parts[k], rows.at[:, pl.ds(k * 2 * cap, 2 * cap), :], sems.at[k])
            for k in range(planes)
        ]
        for copy in copies:
            copy.start()
        for copy in copies:
            copy.wait()

    @pl.when(n == 0)
    def _():
        mine = pl.ds(pl.multiple_of(place[1] * units, units), units)
        for k in range(planes):
            for b in range(2):
                pick = picks(metas[k][b, pl.ds(e, 1), :], cap)
                cal = jnp.sum(jnp.where(pick, metas[k][b, 4:5, :], 0.0), axis=1, keepdims=True)
                at = pl.ds((2 * k + b) * cap, cap)
                scaled[at, :] = (rows[e, at, mine].astype(F32) * cal).astype(BF16)

    width = out.shape[2]
    right = rows[e, :, pl.ds(pl.multiple_of(n * width, width), width)]
    out[0] = lax.dot_general(scaled[...], right, (((0,), (0,)), ((), ())), preferred_element_type=F32)


def gram_blocks(cap, place, metas, parts, width=768):
    planes = len(parts)
    experts, _, depth = parts[0].shape
    units = depth // 4
    total = planes * 2 * cap
    return pl.pallas_call(
        lambda *a: gram_kernel(cap, *a),
        out_shape=jax.ShapeDtypeStruct((experts, units, depth), F32),
        grid=(experts, depth // width),
        in_specs=[SMEM] + [whole(m.shape) for m in metas] + [ANY] * planes,
        out_specs=pl.BlockSpec((1, units, width), lambda e, n: (e, 0, n)),
        scratch_shapes=[
            pltpu.VMEM((experts, total, depth), BF16),
            pltpu.VMEM((total, units), BF16),
            pltpu.SemaphoreType.DMA((planes,)),
        ],
        compiler_params=pltpu.CompilerParams(vmem_limit_bytes=11 * 2**20),
    )(place, *metas, *parts)


CORE = [(c, c ^ 1) for c in range(4)]
ACROSS_Y = [(c, c ^ 2) for c in range(4)]
ACROSS_X = [(e, e ^ 1) for e in range(8)]


def planes_up(k):
    return [(2 * ((z + k) % 4) + x, 2 * z + x) for z in range(4) for x in range(2)]


def over_core(a, what):
    with jax.named_scope(what):
        return lax.ppermute(a, "col", CORE)


def over_y(a, what):
    with jax.named_scope(what):
        return lax.ppermute(a, "col", ACROSS_Y)


def over_x(a, what):
    with jax.named_scope(what):
        return lax.ppermute(a, "expert", ACROSS_X)


def over_z(a, k, what):
    with jax.named_scope(what):
        return lax.ppermute(a, "expert", planes_up(k % 4))


def after(a, *others):
    return lax.optimization_barrier((a, *others))[0]


def by_planes(tokens, routes, route_weight, language, lang_weight, w_gate, w_up, w_down):
    tok, top = routes.shape
    experts = w_gate.shape[0] * lax.axis_size("expert")
    cap = tok * top * 3 // (2 * experts)
    place = jnp.stack([lax.axis_index("expert"), lax.axis_index("col")]).astype(jnp.int32)
    lang_row = jnp.pad(lang_weight, (0, -lang_weight.shape[0] % 128))[None, :]
    n = len(ORDER)
    half = tok // 2
    packed = pack_tokens(tokens, routes, route_weight, language)
    live, metas, parts, sums, kept = {"t0": packed, "lang": lang_row}, {}, {}, {}, None

    def at(turn):
        return ORDER[turn] if 0 <= turn < n else None

    def weigh(k):
        both = [live.pop(f"h{k}"), live.pop(f"hy{k}")]
        far = [over_core(both[0], f"hid_c{k}"), over_core(both[1], f"hid_d{k}")]
        parts[k], *sums[k] = down_rows(cap, place, metas[k], [both[0], far[0], both[1], far[1]], w_down)

    for step in range(n + 2):
        new = {}
        if step == 0:
            new["c0"] = over_core(packed, "tok_c00")
            new["t3"] = over_z(packed, 3, "tok_z3")
            early = over_z(packed, 1, "tok_z1")
        if step == 1:
            new["t2"] = over_z(live["t3"], 3, "tok_z2")
        if step == 2:
            new["t1"] = live.pop("early")
        k = at(step)
        if k is not None:
            new[f"x{k}"], new[f"y{k}"] = over_x(live[f"t{k}"], f"tok_x{k}"), over_y(live[f"t{k}"], f"tok_y{k}")
        k = at(step - 1)
        if k is not None:
            three = [live[f"t{k}"] if k == 0 else live.pop(f"t{k}"), live.pop(f"x{k}"), live.pop(f"y{k}")]
            if step in (1, 2, 3):
                low, high = three[2][:half], three[1][half:tok]
                if step == 1:
                    low, high, new["early"] = lax.optimization_barrier((low, high, early))
                across = [over_x(low, f"tok_dx{k}"), over_y(high, f"tok_dy{k}")]
            else:
                across = [over_x(three[2], f"tok_dx{k}")]
            new[f"near{k}"] = three + across
            if step == n:
                new[f"far{k}"] = [over_core(p, f"tok_c{i}{k}") for i, p in enumerate(three)]
        k = at(step - 2)
        if k is not None:
            near = live.pop(f"near{k}")
            far = [live.pop("c0")] if k == 0 else live.pop(f"far{k}", [])
            far += [over_core(p, f"tok_c{i}{k}") for i, p in enumerate(near) if i >= len(far)]
            made = hidden_rows(cap, not kept, place, live["lang"], tok, near + far, *(kept or (w_gate, w_up)))
            new[f"h{k}"], metas[k] = made[:2]
            kept = kept or made[2:]
        k = at(step - 3)
        if k:
            new[f"hy{k}"] = over_y(live[f"h{k}"], f"hid_y{k}")
        if step == n:
            live.pop("t0")
        if step == n + 1:
            weigh(3)
            new["own3"], new["other3"] = sums.pop(3)
        live = lax.optimization_barrier({**live, **new})

    live["hy1"] = over_y(live["h1"], "hid_y1")
    met3 = over_x(live["other3"], "sum_x3")
    weigh(2)
    met2 = over_x(sums[2][1], "sum_x2")
    live["hy0"] = over_y(after(live["h0"], sums[2][1]), "hid_y0")
    weigh(1)
    met1 = over_x(sums[1][1], "sum_x1")
    back3 = over_z((live["own3"] + met3.astype(F32)).astype(BF16), 1, "sum_z3")
    way2 = (sums[2][0] + met2.astype(F32)).astype(BF16)
    way2 = over_z(way2, 3, "sum_z2")
    weigh(0)
    part = sums[1][0] + met1.astype(F32) + way2.astype(F32)
    last, own_part, other0 = lax.optimization_barrier((part.astype(BF16), parts[0], sums[0][1]))
    met0 = over_x(other0, "sum_x0")
    back1 = over_z(last, 3, "sum_z1")
    out = sums[0][0] + met0.astype(F32) + back3.astype(F32) + back1.astype(F32)
    gram = gram_blocks(cap, place, [metas[k] for k in ORDER], [own_part if k == 0 else parts[k] for k in ORDER])
    return out.astype(BF16), gram


def by_rows(tokens, routes, route_weight, language, lang_weight, w_gate, w_up, w_down):
    tok_rows = routes.shape[0]
    top_count = routes.shape[1]
    local_exp = w_gate.shape[0]
    owners = lax.axis_size("expert")
    experts = local_exp * owners
    capacity = tok_rows * top_count * 3 // (2 * experts)
    expert_ids = jnp.arange(experts, dtype=jnp.int32)
    chosen = routes[:, :, None] == expert_ids[None, None, :]
    hits = jnp.any(chosen, axis=1).astype(jnp.int32)
    coefs = jnp.sum(jnp.where(chosen, route_weight[:, :, None], jnp.zeros((), jnp.float32)), axis=1)
    places = jnp.cumsum(hits, axis=0) - hits
    slot_ids = jnp.arange(capacity, dtype=jnp.int32)
    picks = (hits.T[:, None, :] == 1) & (places.T[:, None, :] == slot_ids[None, :, None])
    row_index = jnp.arange(tok_rows, dtype=jnp.int32)
    slot_token = jnp.sum(jnp.where(picks, row_index[None, None, :], 0), axis=2)
    filled = jnp.any(picks, axis=2)
    lang_table = language[:, None] == jnp.arange(lang_weight.shape[0], dtype=jnp.int32)[None, :]
    calib = jnp.sum(
        jnp.where(lang_table, lang_weight[None, :], jnp.zeros((), jnp.float32)), axis=1
    ).astype(jnp.bfloat16)
    slot_cal = jnp.where(filled, calib[slot_token], jnp.zeros((), jnp.bfloat16)).reshape(
        owners, local_exp, capacity
    )
    slot_coef = jnp.where(
        filled, jnp.take_along_axis(coefs.T, slot_token, axis=1), jnp.zeros((), jnp.float32)
    )
    flat_token = slot_token.reshape(-1)
    flat_filled = filled.reshape(-1)
    whole = lax.all_gather(tokens, "col", axis=1, tiled=True)
    rows = jnp.take(whole, flat_token, axis=0)
    rows = jnp.where(flat_filled[:, None], rows, jnp.zeros((), jnp.bfloat16))
    arrived = lax.all_to_all(
        rows.reshape(owners, local_exp, capacity, whole.shape[1]),
        "expert",
        split_axis=0,
        concat_axis=0,
        tiled=True,
    )
    arrived_cal = lax.all_to_all(slot_cal, "expert", split_axis=0, concat_axis=0, tiled=True)
    gate = jnp.einsum("seck,efk->escf", arrived, w_gate, preferred_element_type=jnp.float32)
    upper = jnp.einsum("seck,efk->escf", arrived, w_up, preferred_element_type=jnp.float32)
    hidden = (jax.nn.silu(gate) * upper).astype(jnp.bfloat16)
    cal_rows = jnp.transpose(arrived_cal, (1, 0, 2))
    scaled = (cal_rows[..., None].astype(jnp.float32) * hidden.astype(jnp.float32)).astype(
        jnp.bfloat16
    )
    d_local = w_down.shape[2]
    piece = lax.all_gather(hidden, "col", axis=3, tiled=True)
    block = jnp.einsum("escu,escv->euv", scaled, piece, preferred_element_type=jnp.float32)
    mixed_now = jnp.einsum("escv,evd->escd", piece, w_down, preferred_element_type=jnp.float32)
    expert_out = mixed_now.astype(jnp.bfloat16)
    returned = lax.all_to_all(expert_out, "expert", split_axis=1, concat_axis=0, tiled=True)
    returned = returned.reshape(experts * capacity, d_local).astype(jnp.float32)
    combined = jnp.zeros((tok_rows, d_local), jnp.float32)
    combined = combined.at[flat_token].add(slot_coef.reshape(-1)[:, None] * returned)
    return (combined.astype(jnp.bfloat16), block)


def solution(mesh):
    in_specs = (
        P("expert", "col"),
        P("expert", None),
        P("expert", None),
        P("expert"),
        P(),
        P("expert", "col", None),
        P("expert", "col", None),
        P("expert", None, "col"),
    )
    out_specs = (P("expert", "col"), P("expert", "col", None))
    body = by_planes if dict(mesh.shape) == {"expert": 8, "col": 4} else by_rows
    return jax.shard_map(body, mesh=mesh, in_specs=in_specs, out_specs=out_specs, check_vma=False)
```

```python
import jax
import jax.numpy as jnp
from jax import lax
from jax.experimental import pallas as pl
from jax.experimental.pallas import tpu as pltpu
from jax.sharding import PartitionSpec as P

F32 = jnp.float32
BF16 = jnp.bfloat16
ORDER = (0, 3, 2, 1)


def whole(shape):
    return pl.BlockSpec(shape, lambda *_: (0,) * len(shape))


ANY = pl.BlockSpec(memory_space=pl.ANY)
SMEM = pl.BlockSpec(memory_space=pltpu.SMEM)
VMEM = pl.BlockSpec(memory_space=pltpu.VMEM)
HBM = pl.BlockSpec(memory_space=pltpu.HBM)


def pack_kernel(tokens, routes, weight, language, out, sem):
    top, tok = routes.shape
    copy = pltpu.make_async_copy(tokens, out.at[pl.ds(0, tok)], sem)
    copy.start()
    out[tok:, :] = jnp.zeros((out.shape[0] - tok, out.shape[1]), BF16)
    out[tok : tok + top, 0:tok] = routes[...].astype(F32).astype(BF16)
    left = weight[...]
    for i in range(1, 4):
        part = left.astype(BF16)
        out[tok : tok + top, i * tok : (i + 1) * tok] = part
        left = left - part.astype(F32)
    out[tok : tok + 1, 4 * tok : 5 * tok] = language[...].astype(F32).astype(BF16)
    copy.wait()


def pack_tokens(tokens, routes, route_weight, language):
    tok, feat = tokens.shape
    return pl.pallas_call(
        pack_kernel,
        out_shape=pltpu.VMEM((tok + 16, feat), BF16),
        in_specs=[HBM, VMEM, VMEM, VMEM],
        out_specs=VMEM,
        scratch_shapes=[pltpu.SemaphoreType.DMA],
    )(in_hbm(tokens), routes.T, route_weight.T, language[None, :])


def fill_routes(place, lang_w, info, meta):
    tok = meta.shape[2]
    top = 8
    lower = (
        lax.broadcasted_iota(jnp.int32, (tok, tok), 0)
        < lax.broadcasted_iota(jnp.int32, (tok, tok), 1)
    ).astype(BF16)
    language_ids = lax.broadcasted_iota(jnp.int32, (lang_w.shape[1], tok), 0).astype(F32)
    lang_column = jnp.broadcast_to(lang_w[...], (tok, lang_w.shape[1])).T
    meta[...] = jnp.zeros_like(meta)
    for b in range(2):
        block = info[b].astype(F32)
        routes, lang = block[0:top, 0:tok], block[0:1, 4 * tok : 5 * tok]
        weight = sum(block[0:top, i * tok : (i + 1) * tok] for i in (1, 2, 3))
        hits = []
        for i in range(2):
            mine = routes == (place[0] * 2 + i).astype(F32)
            hits.append(jnp.max(jnp.where(mine, 1.0, 0.0), axis=0, keepdims=True))
            meta[b, 2 + i : 3 + i, :] = jnp.sum(jnp.where(mine, weight, 0.0), axis=0, keepdims=True)
        hit = jnp.concatenate(hits + [jnp.zeros((6, tok), F32)], axis=0)
        before = jnp.dot(hit.astype(BF16), lower, preferred_element_type=F32)
        meta[b, 0:2, :] = jnp.where(hit > 0.5, before, -1.0)[0:2]
        cal = jnp.sum(jnp.where(language_ids == lang, lang_column, 0.0), axis=0, keepdims=True)
        meta[b, 4:5, :] = cal.astype(BF16).astype(F32)


def picks(slot_row, cap):
    rows = lax.broadcasted_iota(jnp.int32, (cap, slot_row.shape[1]), 0).astype(F32)
    return rows == slot_row


def in_hbm(a):
    return pltpu.with_memory_space_constraint(a, pltpu.HBM)


def held(a):
    return pltpu.with_memory_space_constraint(a, pltpu.VMEM)


def hidden_kernel(cap, first, place, lang_w, *refs):
    if first:
        pieces, (w_gate, w_up, out, meta, gate_held, up_held, x, info, sems, weight_sems) = refs[:-10], refs[-10:]
    else:
        pieces, (gate_held, up_held, out, meta, x, info, sems) = refs[:-7], refs[-7:]
    tok = meta.shape[2]
    feat = x.shape[1] // 4
    half = len(pieces) // 2
    experts = gate_held.shape[0]
    copies, moves = [], []
    for core in range(2):
        row = 0
        for i in range(half):
            src = pieces[core * half + i]
            if src.shape[0] > tok:
                src = src.at[pl.ds(0, tok)]
            b, y = ((0, 0), (1, 0), (0, 1))[i] if i < 3 else (1, 1)
            at = pl.multiple_of((place[1] ^ (core + 2 * y)) * feat, feat)
            dst = x.at[pl.ds(b * tok + row, src.shape[0]), pl.ds(at, feat)]
            if i >= 3:
                row += src.shape[0]
            if core == 0:
                copies.append(pltpu.make_async_copy(src, dst, sems.at[i]))
            else:
                moves.append((src, dst))
    loads = [[] for _ in range(experts)]
    if first:
        for e in range(experts):
            for i, (src, dst) in enumerate(((w_gate, gate_held), (w_up, up_held))):
                loads[e].append(pltpu.make_async_copy(src.at[e], dst.at[e], weight_sems.at[2 * e + i]))
    routes = [
        pltpu.make_async_copy(pieces[b].at[pl.ds(tok, 16)], info.at[b], sems.at[len(pieces) + b]) for b in range(2)
    ]
    for copy in routes + copies + loads[0]:
        copy.start()
    for src, dst in moves:
        dst[...] = src[...]
    for copy in routes + copies + loads[0]:
        copy.wait()
    for later in loads[1:]:
        for copy in later:
            copy.start()
    dims = (((1,), (1,)), ((), ()))
    for e in range(experts):
        for copy in loads[e] if e else []:
            copy.wait()
        gate = lax.dot_general(gate_held[e], x[...], dims, preferred_element_type=F32)
        if e == 0:
            fill_routes(place, lang_w, info, meta)
        up = lax.dot_general(up_held[e], x[...], dims, preferred_element_type=F32)
        hidden = (gate / (1.0 + jnp.exp(-gate)) * up).astype(BF16)
        for b in range(2):
            pick = jnp.where(picks(meta[b, e : e + 1, :], cap), 1.0, 0.0).astype(BF16)
            out[e, b * cap : (b + 1) * cap, :] = lax.dot_general(
                pick, hidden[:, b * tok : (b + 1) * tok], dims, preferred_element_type=F32
            ).astype(BF16)


def hidden_rows(cap, first, place, lang_row, tok, pieces, w_gate, w_up):
    experts, units, depth = w_gate.shape
    outs = (pltpu.VMEM((experts, 2 * cap, units), BF16), jax.ShapeDtypeStruct((2, 8, tok), F32))
    scratch = [
        pltpu.VMEM((2 * tok, depth), BF16),
        pltpu.VMEM((2, 16, depth // 4), BF16),
        pltpu.SemaphoreType.DMA((len(pieces) + 2,)),
    ]
    if first:
        outs += (pltpu.VMEM(w_gate.shape, BF16), pltpu.VMEM(w_up.shape, BF16))
        scratch.append(pltpu.SemaphoreType.DMA((2 * experts,)))
    where = in_hbm if first else held
    return pl.pallas_call(
        lambda *a: hidden_kernel(cap, first, *a),
        out_shape=outs,
        in_specs=[SMEM, VMEM] + [ANY] * (len(pieces) // 2) + [VMEM] * (len(pieces) // 2) + [HBM if first else VMEM] * 2,
        out_specs=(VMEM,) * len(outs),
        scratch_shapes=scratch,
        compiler_params=pltpu.CompilerParams(vmem_limit_bytes=8 * 2**20),
    )(place, lang_row, *map(in_hbm, pieces[: len(pieces) // 2]), *map(held, pieces[len(pieces) // 2 :]), where(w_gate), where(w_up))


def down_kernel(cap, place, meta, made, made_c, made_y, made_d, w_down, rows, own, other, total):
    units = made.shape[2]
    tok = meta.shape[2]
    for i, src in enumerate((made, made_c, made_y, made_d)):
        at = pl.multiple_of((place[1] ^ i) * units, units)
        rows[:, :, pl.ds(at, units)] = src[...]
    for e in range(w_down.shape[0]):
        eo = jnp.dot(rows[e], w_down[e], preferred_element_type=F32)
        for b in range(2):
            pick = picks(meta[b, e : e + 1, :], cap)
            coef = jnp.sum(jnp.where(pick, meta[b, 2 + e : 3 + e, :], 0.0), axis=1, keepdims=True)
            part = (eo[b * cap : (b + 1) * cap] * coef).astype(BF16)
            spread = lax.dot_general(
                jnp.where(pick, 1.0, 0.0).astype(BF16), part, (((0,), (0,)), ((), ())), preferred_element_type=F32
            )
            at = pl.ds(b * tok, tok)
            if e == 0:
                total[at, :] = spread
            elif b == 0:
                own[...] = total[at, :] + spread
            else:
                other[...] = (total[at, :] + spread).astype(BF16)


def down_rows(cap, place, meta, pieces, w_down):
    experts, depth, cols = w_down.shape
    tok = meta.shape[2]
    return pl.pallas_call(
        lambda *a: down_kernel(cap, *a),
        out_shape=(
            pltpu.VMEM((experts, 2 * cap, depth), BF16),
            pltpu.VMEM((tok, cols), F32),
            pltpu.VMEM((tok, cols), BF16),
        ),
        in_specs=[SMEM, VMEM] + [VMEM] * 4 + [VMEM],
        out_specs=(VMEM, VMEM, VMEM),
        scratch_shapes=[pltpu.VMEM((2 * tok, cols), F32)],
        compiler_params=pltpu.CompilerParams(vmem_limit_bytes=8 * 2**20),
    )(place, meta, *map(held, pieces), held(w_down))


def gram_kernel(cap, place, *refs):
    planes = len(refs) // 2 - 1
    metas, parts, (out, scaled) = refs[:planes], refs[planes : 2 * planes], refs[2 * planes :]
    units = scaled.shape[1]
    e, n = pl.program_id(0), pl.program_id(1)

    @pl.when(n == 0)
    def _():
        mine = pl.ds(pl.multiple_of(place[1] * units, units), units)
        for k in range(planes):
            for b in range(2):
                pick = picks(metas[k][b, pl.ds(e, 1), :], cap)
                cal = jnp.sum(jnp.where(pick, metas[k][b, 4:5, :], 0.0), axis=1, keepdims=True)
                at = pl.ds((2 * k + b) * cap, cap)
                scaled[at, :] = (parts[k][e, pl.ds(b * cap, cap), mine].astype(F32) * cal).astype(BF16)

    width = out.shape[2]
    columns = pl.ds(pl.multiple_of(n * width, width), width)
    right = jnp.concatenate([part[e, :, columns] for part in parts], axis=0)
    out[0] = lax.dot_general(scaled[...], right, (((0,), (0,)), ((), ())), preferred_element_type=F32)


def gram_blocks(cap, place, metas, parts, width=768):
    planes = len(parts)
    experts, _, depth = parts[0].shape
    units = depth // 4
    return pl.pallas_call(
        lambda *a: gram_kernel(cap, *a),
        out_shape=jax.ShapeDtypeStruct((experts, units, depth), F32),
        grid=(experts, depth // width),
        in_specs=[SMEM] + [VMEM] * (2 * planes),
        out_specs=pl.BlockSpec((1, units, width), lambda e, n: (e, 0, n)),
        scratch_shapes=[pltpu.VMEM((planes * 2 * cap, units), BF16)],
        compiler_params=pltpu.CompilerParams(vmem_limit_bytes=14 * 2**20),
    )(place, *metas, *map(held, parts))


CORE = [(c, c ^ 1) for c in range(4)]
ACROSS_Y = [(c, c ^ 2) for c in range(4)]
ACROSS_X = [(e, e ^ 1) for e in range(8)]


def planes_up(k):
    return [(2 * ((z + k) % 4) + x, 2 * z + x) for z in range(4) for x in range(2)]


def over_core(a, what):
    with jax.named_scope(what):
        return lax.ppermute(a, "col", CORE)


def over_y(a, what):
    with jax.named_scope(what):
        return lax.ppermute(a, "col", ACROSS_Y)


def over_x(a, what):
    with jax.named_scope(what):
        return lax.ppermute(a, "expert", ACROSS_X)


def over_z(a, k, what):
    with jax.named_scope(what):
        return lax.ppermute(a, "expert", planes_up(k % 4))


def after(a, *others):
    return lax.optimization_barrier((a, *others))[0]


def by_planes(tokens, routes, route_weight, language, lang_weight, w_gate, w_up, w_down):
    tok, top = routes.shape
    experts = w_gate.shape[0] * lax.axis_size("expert")
    cap = tok * top * 3 // (2 * experts)
    place = jnp.stack([lax.axis_index("expert"), lax.axis_index("col")]).astype(jnp.int32)
    lang_row = jnp.pad(lang_weight, (0, -lang_weight.shape[0] % 128))[None, :]
    n = len(ORDER)
    half = tok // 2
    packed = pack_tokens(tokens, routes, route_weight, language)
    live, metas, parts, sums, kept = {"t0": packed, "lang": lang_row}, {}, {}, {}, None

    def at(turn):
        return ORDER[turn] if 0 <= turn < n else None

    def weigh(k):
        both = [live.pop(f"h{k}"), live.pop(f"hy{k}")]
        far = [over_core(both[0], f"hid_c{k}"), over_core(both[1], f"hid_d{k}")]
        parts[k], *sums[k] = down_rows(cap, place, metas[k], [both[0], far[0], both[1], far[1]], w_down)

    for step in range(n + 2):
        new = {}
        if step == 0:
            new["c0"] = over_core(packed, "tok_c00")
            new["t3"] = over_z(packed, 3, "tok_z3")
            early = over_z(packed, 1, "tok_z1")
        if step == 1:
            new["t2"] = over_z(live["t3"], 3, "tok_z2")
        if step == 2:
            new["t1"] = live.pop("early")
        k = at(step)
        if k is not None:
            new[f"x{k}"], new[f"y{k}"] = over_x(live[f"t{k}"], f"tok_x{k}"), over_y(live[f"t{k}"], f"tok_y{k}")
        k = at(step - 1)
        if k is not None:
            three = [live[f"t{k}"] if k == 0 else live.pop(f"t{k}"), live.pop(f"x{k}"), live.pop(f"y{k}")]
            if step in (1, 2, 3):
                low, high = three[2][:half], three[1][half:tok]
                if step == 1:
                    low, high, new["early"] = lax.optimization_barrier((low, high, early))
                across = [over_x(low, f"tok_dx{k}"), over_y(high, f"tok_dy{k}")]
            else:
                across = [over_x(three[2], f"tok_dx{k}")]
            new[f"near{k}"] = three + across
            if step == n:
                new[f"far{k}"] = [over_core(p, f"tok_c{i}{k}") for i, p in enumerate(three)]
        k = at(step - 2)
        if k is not None:
            near = live.pop(f"near{k}")
            far = [live.pop("c0")] if k == 0 else live.pop(f"far{k}", [])
            far += [over_core(p, f"tok_c{i}{k}") for i, p in enumerate(near) if i >= len(far)]
            made = hidden_rows(cap, not kept, place, live["lang"], tok, near + far, *(kept or (w_gate, w_up)))
            new[f"h{k}"], metas[k] = made[:2]
            kept = kept or made[2:]
        k = at(step - 3)
        if k:
            new[f"hy{k}"] = over_y(live[f"h{k}"], f"hid_y{k}")
        if step == n:
            live.pop("t0")
        if step == n + 1:
            weigh(3)
            new["own3"], new["other3"] = sums.pop(3)
        live = lax.optimization_barrier({**live, **new})

    live["hy1"] = over_y(live["h1"], "hid_y1")
    met3 = over_x(live["other3"], "sum_x3")
    weigh(2)
    met2 = over_x(sums[2][1], "sum_x2")
    live["hy0"] = over_y(after(live["h0"], sums[2][1]), "hid_y0")
    weigh(1)
    met1 = over_x(sums[1][1], "sum_x1")
    back3 = over_z((live["own3"] + met3.astype(F32)).astype(BF16), 1, "sum_z3")
    way2 = (sums[2][0] + met2.astype(F32)).astype(BF16)
    way2 = over_z(way2, 3, "sum_z2")
    weigh(0)
    part = sums[1][0] + met1.astype(F32) + way2.astype(F32)
    last, own_part, other0 = lax.optimization_barrier((part.astype(BF16), parts[0], sums[0][1]))
    met0 = over_x(other0, "sum_x0")
    back1 = over_z(last, 3, "sum_z1")
    out = sums[0][0] + met0.astype(F32) + back3.astype(F32) + back1.astype(F32)
    gram = gram_blocks(cap, place, [metas[k] for k in ORDER], [own_part if k == 0 else parts[k] for k in ORDER])
    return out.astype(BF16), gram


def by_rows(tokens, routes, route_weight, language, lang_weight, w_gate, w_up, w_down):
    tok_rows = routes.shape[0]
    top_count = routes.shape[1]
    local_exp = w_gate.shape[0]
    owners = lax.axis_size("expert")
    experts = local_exp * owners
    capacity = tok_rows * top_count * 3 // (2 * experts)
    expert_ids = jnp.arange(experts, dtype=jnp.int32)
    chosen = routes[:, :, None] == expert_ids[None, None, :]
    hits = jnp.any(chosen, axis=1).astype(jnp.int32)
    coefs = jnp.sum(jnp.where(chosen, route_weight[:, :, None], jnp.zeros((), jnp.float32)), axis=1)
    places = jnp.cumsum(hits, axis=0) - hits
    slot_ids = jnp.arange(capacity, dtype=jnp.int32)
    picks = (hits.T[:, None, :] == 1) & (places.T[:, None, :] == slot_ids[None, :, None])
    row_index = jnp.arange(tok_rows, dtype=jnp.int32)
    slot_token = jnp.sum(jnp.where(picks, row_index[None, None, :], 0), axis=2)
    filled = jnp.any(picks, axis=2)
    lang_table = language[:, None] == jnp.arange(lang_weight.shape[0], dtype=jnp.int32)[None, :]
    calib = jnp.sum(
        jnp.where(lang_table, lang_weight[None, :], jnp.zeros((), jnp.float32)), axis=1
    ).astype(jnp.bfloat16)
    slot_cal = jnp.where(filled, calib[slot_token], jnp.zeros((), jnp.bfloat16)).reshape(
        owners, local_exp, capacity
    )
    slot_coef = jnp.where(
        filled, jnp.take_along_axis(coefs.T, slot_token, axis=1), jnp.zeros((), jnp.float32)
    )
    flat_token = slot_token.reshape(-1)
    flat_filled = filled.reshape(-1)
    whole = lax.all_gather(tokens, "col", axis=1, tiled=True)
    rows = jnp.take(whole, flat_token, axis=0)
    rows = jnp.where(flat_filled[:, None], rows, jnp.zeros((), jnp.bfloat16))
    arrived = lax.all_to_all(
        rows.reshape(owners, local_exp, capacity, whole.shape[1]),
        "expert",
        split_axis=0,
        concat_axis=0,
        tiled=True,
    )
    arrived_cal = lax.all_to_all(slot_cal, "expert", split_axis=0, concat_axis=0, tiled=True)
    gate = jnp.einsum("seck,efk->escf", arrived, w_gate, preferred_element_type=jnp.float32)
    upper = jnp.einsum("seck,efk->escf", arrived, w_up, preferred_element_type=jnp.float32)
    hidden = (jax.nn.silu(gate) * upper).astype(jnp.bfloat16)
    cal_rows = jnp.transpose(arrived_cal, (1, 0, 2))
    scaled = (cal_rows[..., None].astype(jnp.float32) * hidden.astype(jnp.float32)).astype(
        jnp.bfloat16
    )
    d_local = w_down.shape[2]
    piece = lax.all_gather(hidden, "col", axis=3, tiled=True)
    block = jnp.einsum("escu,escv->euv", scaled, piece, preferred_element_type=jnp.float32)
    mixed_now = jnp.einsum("escv,evd->escd", piece, w_down, preferred_element_type=jnp.float32)
    expert_out = mixed_now.astype(jnp.bfloat16)
    returned = lax.all_to_all(expert_out, "expert", split_axis=1, concat_axis=0, tiled=True)
    returned = returned.reshape(experts * capacity, d_local).astype(jnp.float32)
    combined = jnp.zeros((tok_rows, d_local), jnp.float32)
    combined = combined.at[flat_token].add(slot_coef.reshape(-1)[:, None] * returned)
    return (combined.astype(jnp.bfloat16), block)


def solution(mesh):
    in_specs = (
        P("expert", "col"),
        P("expert", None),
        P("expert", None),
        P("expert"),
        P(),
        P("expert", "col", None),
        P("expert", "col", None),
        P("expert", None, "col"),
    )
    out_specs = (P("expert", "col"), P("expert", "col", None))
    body = by_planes if dict(mesh.shape) == {"expert": 8, "col": 4} else by_rows
    return jax.shard_map(body, mesh=mesh, in_specs=in_specs, out_specs=out_specs, check_vma=False)
```
